256 devices in a mesh: ctx: 32 (over y_lo, z, core), ch: 8 (over x, y_hi).
Axes of the slice: x: 4, y: 4 (y_hi: 2, y_lo: 2; y = y_hi * 2 + y_lo), z: 8, core: 2. Of those that a mesh axis runs over, the one named last changes fastest.
Arguments:
- inputs: bfloat16 [8192, 4096], P('ctx', 'ch'), may hold values from -6 to 6
- in_weight: bfloat16 [4096, 3, 2048], P(None, None, 'ch'), may hold values from -0.09375 to 0.09375
- short_kernel: float32 [3, 3, 2048], P(None, None, 'ch'), may hold values from -3 to 3
- long_filter: float32 [8192, 2048], P('ctx', 'ch'), may hold values from -4 to 4
- skip_gain: float32 [2048], P('ch'), may hold values from -4 to 4
- out_weight: bfloat16 [2048, 4096], P(None, 'ch'), may hold values from -0.125 to 0.125
Outputs:
- mixed: bfloat16 [8192, 4096], P('ctx', 'ch')
The draws below stay inside these ranges and needn't reach their ends.
All inputs are finite; a program needn't handle non-finite values.
Results may differ from the reference program's by a relative error of at most 0.005.
Values may be sent and summed in bfloat16 or wider, within the bound.
A program may use at most 64 MiB of HBM per device.

```python
import jax
import jax.numpy as jnp

D = 4096
SLAB = 2048
L = 8192


def draw_long_filter(key, part):
    key = jax.random.fold_in(key, 11)
    rate_key, rough_key = jax.random.split(key, 2)
    length = L * 1.0
    rate = jnp.exp(jax.random.uniform(rate_key, (1, SLAB), jnp.float32, jnp.log(0.5 / length), jnp.log(1.0 / 30.0)))
    rough = jnp.clip(jax.random.normal(rough_key, (L, SLAB), jnp.float32), -4.0, 4.0)
    steps = jnp.arange(L, dtype=jnp.float32)[:, None]
    amplitude = jnp.sqrt(jnp.expm1(-2.0 * rate) / jnp.expm1(-2.0 * rate * length))
    return rough * amplitude * jnp.exp(-rate * steps)


def shard_levels(rng, dims, pieces, least, high):
    gain = 1.0
    for position, shards_of in pieces:
        steps = jax.random.uniform(jax.random.fold_in(jax.random.fold_in(rng, 6), position), (shards_of,), jnp.float32, least / len(pieces), high / len(pieces))
        gain = gain * jnp.repeat(jnp.exp(steps), dims[position] // shards_of).reshape((-1,) + (1,) * (len(dims) - 1 - position))
    return gain


def noise(rng, extent, spread, reach, pieces=(), held_as=jnp.bfloat16):
    result = jax.random.normal(rng, extent, jnp.float32) * spread
    if len(pieces) > 0:
        result = shard_levels(rng, extent, pieces, -0.22, 0.18) * result
    return jnp.clip(result, min=-reach, max=reach).astype(held_as)


def setup_inputs(seed: int = 0) -> dict:
    seeds = jax.random.split(jax.random.key(seed), 7)
    inputs = noise(seeds[0], (L, D), 1.0, 6.0, ((0, 32), (1, 8)))
    in_weight = noise(seeds[1], (D, 3, SLAB), D ** -0.5, 0.09375, ((2, 8),))
    short_kernel = noise(seeds[2], (3, 3, SLAB), 0.6, 3.0, ((2, 8),), jnp.float32)
    long_filter = draw_long_filter(jax.random.fold_in(seeds[6], 71), 0)
    skip_gain = noise(seeds[4], (SLAB,), 1.0, 4.0, ((0, 8),), jnp.float32)
    out_weight = noise(seeds[5], (SLAB, D), SLAB ** -0.5, 0.125, ((1, 8),))
    return {"inputs": inputs, "in_weight": in_weight, "short_kernel": short_kernel, "long_filter": long_filter, "skip_gain": skip_gain, "out_weight": out_weight}


def reference(inputs, in_weight, short_kernel, long_filter, skip_gain, out_weight):
    projected = jnp.dot(inputs, in_weight.reshape(D, 3 * SLAB), preferred_element_type=jnp.float32)
    projected = projected.reshape(L, 3, SLAB)
    padded = jnp.pad(projected, ((2, 0), (0, 0), (0, 0)))
    streams = short_kernel[0] * padded[2:] + short_kernel[1] * padded[1:-1] + short_kernel[2] * padded[:-2]
    first_gate = streams[:, 0]
    second_gate = streams[:, 1]
    value = streams[:, 2]
    gated = first_gate * value
    spectrum = jnp.fft.rfft(gated, n=2 * L, axis=0) * jnp.fft.rfft(long_filter, n=2 * L, axis=0)
    conv = jnp.fft.irfft(spectrum, n=2 * L, axis=0)[:L].astype(jnp.float32)
    gated_out = (second_gate * (conv + skip_gain * gated)).astype(jnp.bfloat16)
    return jnp.dot(gated_out, out_weight, preferred_element_type=jnp.float32).astype(jnp.bfloat16)
```

```python
import functools
import math

import jax
import jax.numpy as jnp
import ml_dtypes
import numpy as np
from jax import lax
from jax.experimental import pallas as pl
from jax.experimental.pallas import tpu as pltpu
from jax.sharding import PartitionSpec as P

MESH = pl.DeviceIdType.MESH
BF16 = jnp.bfloat16
F32 = jnp.float32
LANES = 128
OWN = 8


def halves(table):
    high = table.astype(ml_dtypes.bfloat16)
    low = (table - high.astype(np.float64)).astype(ml_dtypes.bfloat16)
    return np.stack([high, low])


def tables(length):
    rows = length // LANES
    k1 = np.arange(rows)[:, None] + 0.5
    n1 = np.arange(rows)[None, :]
    n2 = np.arange(LANES)[None, :]
    k2 = np.arange(LANES)[:, None]
    outer = 2.0 * math.pi * k1 * n1 / (2 * rows)
    first = np.concatenate([np.cos(outer), -np.sin(outer)], 0)
    turn = 2.0 * math.pi * k1 * n2 / (2 * length)
    twist = np.stack([np.cos(turn), -np.sin(turn)]).astype(np.float32)
    inner = 2.0 * math.pi * k2 * n2 / LANES
    cosine, sine = np.cos(inner), np.sin(inner)
    second = np.block([[cosine, -sine], [sine, cosine]])
    back = np.block([[cosine, sine], [-sine, cosine]])
    return (
        halves(first),
        halves(first.T / length),
        np.concatenate([halves(second), halves(back)]),
        twist,
    )


def split(value):
    high = value.astype(BF16)
    return high, (value - high.astype(F32)).astype(BF16)


def dot(left, right):
    return jnp.dot(left, right, preferred_element_type=F32)


def kernel(nctx, nch, ny, *refs):
    (
        x_hbm, w_hbm, taps_hbm, filt_hbm, skip_hbm, wo_hbm,
        first_hbm, last_hbm, mid_hbm, twist_hbm,
        out_ref,
        xg, w, taps, filt, skip, wo, first, last, mid, twist,
        proj, gate, gated, hsend, hrecv, gsend, grecv, csend, crecv, yg,
        line, spec, hspec, dhi, dlo, acc,
        local_sem, x_send, x_recv, halo_sem, h_sem, g_sem, c_sem, y_send, y_recv,
    ) = refs
    ctx = lax.axis_index("ctx")
    ch = lax.axis_index("ch")
    rows, feats = x_hbm.shape
    chans = filt_hbm.shape[1]
    k1 = first_hbm.shape[2]

    def peer(step):
        nx = nch // ny
        dx = (step // ny) % nx
        dx = dx ^ (dx // 2)
        dy = step % ny
        x, y = ch // ny, ch % ny
        yy = (y + dy) % ny
        return ((x + dx) % nx) * ny + yy, ((x + nx - dx) % nx) * ny + yy

    def loads():
        pairs = (
            (x_hbm, xg.at[ch]), (filt_hbm, filt), (first_hbm, first), (mid_hbm, mid), (twist_hbm, twist),
            (last_hbm, last), (taps_hbm, taps), (skip_hbm, skip), (w_hbm, w), (wo_hbm, wo),
        )
        return [pltpu.make_async_copy(s, d, local_sem.at[i]) for i, (s, d) in enumerate(pairs)]

    local = loads()
    for copy in local:
        copy.start()

    barrier = pltpu.get_barrier_semaphore()

    def greet_ctx(d, carry):
        pl.semaphore_signal(barrier, inc=1, device_id={"ctx": (ctx + d) % nctx}, device_id_type=MESH)
        return carry

    def greet_ch(d, carry):
        pl.semaphore_signal(barrier, inc=1, device_id={"ch": (ch + d) % nch}, device_id_type=MESH)
        return carry

    lax.fori_loop(1, nch, greet_ch, 0)
    lax.fori_loop(1, nctx, greet_ctx, 0)
    pl.semaphore_wait(barrier, nctx + nch - 2)


    def gather(source, slots, send, recv, step):
        to, _ = peer(step)
        return pltpu.make_async_remote_copy(
            src_ref=source, dst_ref=slots.at[ch], send_sem=send.at[step], recv_sem=recv.at[step],
            device_id={"ch": to}, device_id_type=MESH,
        )

    def x_start(step, carry):
        gather(x_hbm, xg, x_send, x_recv, step).start()
        return carry

    lax.fori_loop(1, nch, x_start, 0)


    def exchange(send, recv, sem):
        def body(d, carry):
            to = (ctx + d) % nctx
            pltpu.make_async_remote_copy(
                src_ref=send.at[to], dst_ref=recv.at[ctx], send_sem=sem.at[0], recv_sem=sem.at[1],
                device_id={"ctx": to}, device_id_type=MESH,
            ).start()
            return carry

        lax.fori_loop(1, nctx, body, 0)
        recv[pl.ds(ctx, 1)] = send[pl.ds(ctx, 1)]

    def whole(send, sem):
        part = send.at[pl.ds(0, nctx - 1)]
        return pltpu.make_async_copy(part, part, sem)

    def to_parts(block):
        turned = block.T.reshape(nctx, OWN, rows)
        return jnp.concatenate([turned[:, :, :LANES], turned[:, :, LANES:]], axis=1)

    def forward(result, exact):
        block = jnp.concatenate([line[pl.ds(c, k1, stride=OWN), :] for c in range(OWN)], axis=1)
        high, low = split(block)
        turned = dot(first[0], high) + dot(first[1], high)
        if not exact:
            turned = turned + dot(first[0], low)
        for c in range(OWN):
            real = turned[:k1, c * LANES : (c + 1) * LANES]
            imag = turned[k1:, c * LANES : (c + 1) * LANES]
            at = pl.ds(c * k1, k1)
            dhi[at, :LANES], dlo[at, :LANES] = split(real * twist[0] - imag * twist[1])
            dhi[at, LANES:], dlo[at, LANES:] = split(real * twist[1] + imag * twist[0])
        result[...] = dot(dhi[...], mid[0]) + dot(dhi[...], mid[1]) + dot(dlo[...], mid[0])

    def backward():
        xr, xi = spec[:, :LANES], spec[:, LANES:]
        hr, hi = hspec[:, :LANES], hspec[:, LANES:]
        dhi[:, :LANES], dlo[:, :LANES] = split(xr * hr - xi * hi)
        dhi[:, LANES:], dlo[:, LANES:] = split(xr * hi + xi * hr)
        spec[...] = dot(dhi[...], mid[2]) + dot(dhi[...], mid[3]) + dot(dlo[...], mid[2])
        cols = []
        for c in range(OWN):
            at = pl.ds(c * k1, k1)
            real, imag = spec[at, :LANES], spec[at, LANES:]
            cols.append(
                jnp.concatenate([real * twist[0] + imag * twist[1], imag * twist[0] - real * twist[1]], axis=0)
            )
        high, low = split(jnp.concatenate(cols, axis=1))
        signal = dot(last[0], high) + dot(last[1], high) + dot(last[0], low)
        for c in range(OWN):
            line[pl.ds(c, k1, stride=OWN), :] = signal[:, c * LANES : (c + 1) * LANES]

    for copy in local[1:6]:
        copy.wait()
    hsend[...] = to_parts(filt[...])
    exchange(hsend, hrecv, h_sem)
    whole(hsend, h_sem.at[1]).wait()
    line[...] = hrecv[...].reshape(line.shape)
    forward(hspec, False)
    whole(hsend, h_sem.at[0]).wait()

    for copy in local[6:] + local[:1]:
        copy.wait()
    top = 8

    def project(step, carry):
        _, src = peer(step)

        @pl.when(step > 0)
        def _():
            pltpu.make_async_remote_copy(
                src_ref=x_hbm, dst_ref=xg.at[src], send_sem=x_send.at[step], recv_sem=x_recv.at[step],
                device_id={"ch": src}, device_id_type=MESH,
            ).wait_recv()

        part = xg[src]
        at = pl.ds(pl.multiple_of(src * feats, feats), feats)
        for s in range(3):
            cols = pl.ds(s * chans, chans)
            proj[top:, cols] += dot(part, w[s, at, :])
        return carry

    proj[top:] = jnp.zeros((rows, 3 * chans), F32)
    lax.fori_loop(0, nch, project, 0)
    halo = pltpu.make_async_remote_copy(
        src_ref=proj.at[pl.ds(rows, top)], dst_ref=proj.at[pl.ds(0, top)],
        send_sem=halo_sem.at[0], recv_sem=halo_sem.at[1],
        device_id={"ctx": (ctx + 1) % nctx}, device_id_type=MESH,
    )
    halo.start()
    halo.wait()
    proj[:top] = jnp.where(ctx == 0, 0.0, proj[:top])

    def stream(s):
        cols = pl.ds(s * chans, chans)
        return (
            taps[0, s : s + 1, :] * proj[top:, cols]
            + taps[1, s : s + 1, :] * proj[pl.ds(top - 1, rows), cols]
            + taps[2, s : s + 1, :] * proj[pl.ds(top - 2, rows), cols]
        )

    gated[...] = stream(0) * stream(2)
    gsend[...] = to_parts(gated[...]).astype(BF16)
    exchange(gsend, grecv, g_sem)
    gate[...] = stream(1)
    whole(gsend, g_sem.at[1]).wait()

    line[...] = grecv[...].astype(F32).reshape(line.shape)
    forward(spec, True)
    backward()
    csend[...] = line[...].reshape(csend.shape).astype(BF16)
    exchange(csend, crecv, c_sem)
    whole(csend, c_sem.at[1]).wait()
    back = crecv[...].astype(F32)
    for part in range(2):
        at = pl.ds(part * LANES, LANES)
        conv = back[:, part * OWN : (part + 1) * OWN, :].reshape(chans, LANES).T
        mixed = gate[at, :] * (conv + skip[...] * gated[at, :])
        yg[ch, at, :] = mixed.astype(BF16)

    def y_start(step, carry):
        gather(yg.at[ch], yg, y_send, y_recv, step).start()
        return carry

    lax.fori_loop(1, nch, y_start, 0)

    def mix(step, carry):
        _, src = peer(step)

        @pl.when(step > 0)
        def _():
            pltpu.make_async_remote_copy(
                src_ref=yg.at[ch], dst_ref=yg.at[src], send_sem=y_send.at[step], recv_sem=y_recv.at[step],
                device_id={"ch": src}, device_id_type=MESH,
            ).wait_recv()

        at = pl.ds(pl.multiple_of(src * chans, chans), chans)
        acc[...] += dot(yg[src], wo[at, :])
        return carry

    acc[...] = jnp.zeros_like(acc)
    lax.fori_loop(0, nch, mix, 0)
    out_ref[...] = acc[...].astype(BF16)

    def drain(step, carry):
        gather(x_hbm, xg, x_send, x_recv, step).wait_send()
        gather(yg.at[ch], yg, y_send, y_recv, step).wait_send()
        return carry

    lax.fori_loop(1, nch, drain, 0)
    whole(gsend, g_sem.at[0]).wait()
    whole(csend, c_sem.at[0]).wait()


def shards(nctx, nch, inputs, in_weight, short_kernel, long_filter, skip_gain, out_weight):
    rows, feats = inputs.shape
    width, _, chans = in_weight.shape
    mixed = out_weight.shape[1]
    length = rows * nctx
    consts = [jnp.asarray(t) for t in tables(length)]
    k1 = length // LANES
    operands = [
        inputs, jnp.transpose(in_weight, (1, 0, 2)), short_kernel, long_filter,
        skip_gain.reshape(1, chans), out_weight, *consts,
    ]
    vm = pltpu.VMEM
    parts = (nctx, 2 * OWN, LANES)
    scratch = [
        vm((nch, rows, feats), BF16), vm((3, width, chans), BF16), vm(short_kernel.shape, F32),
        vm((rows, chans), F32), vm((1, chans), F32), vm(out_weight.shape, BF16),
        *[vm(c.shape, c.dtype) for c in consts],
        vm((rows + 8, 3 * chans), F32), vm((rows, chans), F32), vm((rows, chans), F32),
        vm(parts, F32), vm(parts, F32), vm(parts, BF16), vm(parts, BF16), vm(parts, BF16), vm(parts, BF16),
        vm((nch, rows, chans), BF16),
        vm((k1 * OWN, LANES), F32), vm((k1 * OWN, 2 * LANES), F32), vm((k1 * OWN, 2 * LANES), F32),
        vm((k1 * OWN, 2 * LANES), BF16), vm((k1 * OWN, 2 * LANES), BF16), vm((rows, mixed), F32),
    ]
    dma = pltpu.SemaphoreType.DMA
    sems = [dma((10,)), dma((nch,)), dma((nch,)), dma((2,)), dma((2,)), dma((2,)), dma((2,)), dma((nch,)), dma((nch,))]
    return pl.pallas_call(
        functools.partial(kernel, nctx, nch, 2),
        out_shape=jax.ShapeDtypeStruct((rows, mixed), BF16),
        in_specs=[pl.BlockSpec(memory_space=pl.ANY)] * len(operands),
        out_specs=pl.BlockSpec(memory_space=pltpu.VMEM),
        scratch_shapes=scratch + sems,
        compiler_params=pltpu.CompilerParams(
            collective_id=0, has_side_effects=True, vmem_limit_bytes=40 * 1024 * 1024
        ),
    )(*operands)


def solution(mesh):
    placed = (
        P("ctx", "ch"),
        P(None, None, "ch"),
        P(None, None, "ch"),
        P("ctx", "ch"),
        P("ch"),
        P(None, "ch"),
    )
    body = functools.partial(shards, mesh.shape["ctx"], mesh.shape["ch"])
    return jax.shard_map(body, mesh=mesh, in_specs=placed, out_specs=P("ctx", "ch"), check_vma=False)
```

```python
import functools
import math

import jax
import jax.numpy as jnp
import ml_dtypes
import numpy as np
from jax import lax
from jax.experimental import pallas as pl
from jax.experimental.pallas import tpu as pltpu
from jax.sharding import PartitionSpec as P

MESH = pl.DeviceIdType.MESH
BF16 = jnp.bfloat16
F32 = jnp.float32
LANES = 128
OWN = 8


def halves(table):
    high = table.astype(ml_dtypes.bfloat16)
    low = (table - high.astype(np.float64)).astype(ml_dtypes.bfloat16)
    return np.stack([high, low])


def tables(length):
    rows = length // LANES
    k1 = np.arange(rows)[:, None] + 0.5
    n1 = np.arange(rows)[None, :]
    n2 = np.arange(LANES)[None, :]
    k2 = np.arange(LANES)[:, None]
    outer = 2.0 * math.pi * k1 * n1 / (2 * rows)
    first = np.concatenate([np.cos(outer), -np.sin(outer)], 0)
    turn = 2.0 * math.pi * k1 * n2 / (2 * length)
    twist = np.stack([np.cos(turn), -np.sin(turn)]).astype(np.float32)
    inner = 2.0 * math.pi * k2 * n2 / LANES
    cosine, sine = np.cos(inner), np.sin(inner)
    second = np.block([[cosine, -sine], [sine, cosine]])
    back = np.block([[cosine, sine], [-sine, cosine]])
    return (
        halves(first),
        halves(first.T / length),
        np.concatenate([halves(second), halves(back)]),
        twist,
    )


def split(value):
    high = value.astype(BF16)
    return high, (value - high.astype(F32)).astype(BF16)


def dot(left, right):
    return jnp.dot(left, right, preferred_element_type=F32)


def kernel(nctx, nch, ny, *refs):
    (
        x_hbm, w_hbm, taps_hbm, filt_hbm, skip_hbm, wo_hbm,
        first_hbm, last_hbm, mid_hbm, twist_hbm,
        out_ref,
        xg, w, taps, filt, skip, wo, first, last, mid, twist,
        proj, gate, gated, hsend, hrecv, gsend, grecv, csend, crecv, yg,
        line, spec, hspec, dhi, dlo, acc,
        local_sem, x_send, x_recv, halo_sem, h_sem, g_sem, c_sem, y_send, y_recv,
    ) = refs
    ctx = lax.axis_index("ctx")
    ch = lax.axis_index("ch")
    rows, feats = x_hbm.shape
    chans = filt_hbm.shape[1]
    k1 = first_hbm.shape[2]

    nx = nch // ny
    half = rows // 2

    def at_ch(dx, dy):
        return ((ch // ny + dx) % nx) * ny + (ch % ny + dy) % ny

    own, plus, minus, two = at_ch(0, 0), at_ch(1, 0), at_ch(nx - 1, 0), at_ch(2, 0)
    own2, plus2, minus2, two2 = at_ch(0, 1), at_ch(1, 1), at_ch(nx - 1, 1), at_ch(2, 1)

    def loads():
        pairs = (
            (x_hbm, xg.at[ch]), (filt_hbm, filt), (first_hbm, first), (mid_hbm, mid), (twist_hbm, twist),
            (last_hbm, last), (taps_hbm, taps), (skip_hbm, skip), (w_hbm, w), (wo_hbm, wo),
        )
        return [pltpu.make_async_copy(s, d, local_sem.at[i]) for i, (s, d) in enumerate(pairs)]

    local = loads()
    for copy in local:
        copy.start()

    barrier = pltpu.get_barrier_semaphore()

    def greet_ctx(d, carry):
        pl.semaphore_signal(barrier, inc=1, device_id={"ctx": (ctx + d) % nctx}, device_id_type=MESH)
        return carry

    def greet_ch(d, carry):
        pl.semaphore_signal(barrier, inc=1, device_id={"ch": (ch + d) % nch}, device_id_type=MESH)
        return carry

    lax.fori_loop(1, nch, greet_ch, 0)
    lax.fori_loop(1, nctx, greet_ctx, 0)
    pl.semaphore_wait(barrier, nctx + nch - 2)


    def gather(source, slots, send, recv):
        started = []

        def piece(block, h):
            return slots.at[block, pl.ds(h * half, half)]

        def push(block, h, to, src=None):
            copy = pltpu.make_async_remote_copy(
                src_ref=piece(block, h) if src is None else src.at[pl.ds(h * half, half)],
                dst_ref=piece(block, h), send_sem=send.at[len(started)], recv_sem=recv.at[block, h],
                device_id={"ch": to}, device_id_type=MESH,
            )
            copy.start()
            started.append(copy)

        def pull(block, h):
            pltpu.make_async_remote_copy(
                src_ref=piece(block, h), dst_ref=piece(block, h), send_sem=send.at[0], recv_sem=recv.at[block, h],
                device_id={"ch": own2}, device_id_type=MESH,
            ).wait_recv()

        def begin():
            for h, to in ((0, own2), (0, plus), (1, minus), (1, own2), (1, plus), (0, minus)):
                push(own, h, to, source)

        def forward_first():
            pull(own2, 0), push(own2, 0, plus)
            pull(own2, 1), push(own2, 1, minus)
            pull(minus, 0), push(minus, 0, plus)
            pull(plus, 1), push(plus, 1, minus)
            pull(minus, 1), push(minus, 1, own2)
            pull(plus, 0), push(plus, 0, own2)

        def forward_second():
            pull(minus2, 0), push(minus2, 0, plus)
            pull(plus2, 1), push(plus2, 1, minus)

        def finish():
            for copy in started:
                copy.wait_send()

        return begin, forward_first, forward_second, pull, finish

    x_begin, x_first, x_second, x_pull, x_finish = gather(x_hbm, xg, x_send, x_recv)
    x_begin()


    def exchange(send, recv, sem):
        def body(d, carry):
            to = (ctx + d) % nctx
            pltpu.make_async_remote_copy(
                src_ref=send.at[to], dst_ref=recv.at[ctx], send_sem=sem.at[0], recv_sem=sem.at[1],
                device_id={"ctx": to}, device_id_type=MESH,
            ).start()
            return carry

        lax.fori_loop(1, nctx, body, 0)
        recv[pl.ds(ctx, 1)] = send[pl.ds(ctx, 1)]

    def whole(send, sem):
        part = send.at[pl.ds(0, nctx - 1)]
        return pltpu.make_async_copy(part, part, sem)

    def to_parts(block):
        turned = block.T.reshape(nctx, OWN, rows)
        return jnp.concatenate([turned[:, :, :LANES], turned[:, :, LANES:]], axis=1)

    def forward(result, exact):
        block = jnp.concatenate([line[pl.ds(c, k1, stride=OWN), :] for c in range(OWN)], axis=1)
        high, low = split(block)
        turned = dot(first[0], high) + dot(first[1], high)
        if not exact:
            turned = turned + dot(first[0], low)
        for c in range(OWN):
            real = turned[:k1, c * LANES : (c + 1) * LANES]
            imag = turned[k1:, c * LANES : (c + 1) * LANES]
            at = pl.ds(c * k1, k1)
            dhi[at, :LANES], dlo[at, :LANES] = split(real * twist[0] - imag * twist[1])
            dhi[at, LANES:], dlo[at, LANES:] = split(real * twist[1] + imag * twist[0])
        result[...] = dot(dhi[...], mid[0]) + dot(dhi[...], mid[1]) + dot(dlo[...], mid[0])

    def backward():
        xr, xi = spec[:, :LANES], spec[:, LANES:]
        hr, hi = hspec[:, :LANES], hspec[:, LANES:]
        dhi[:, :LANES], dlo[:, :LANES] = split(xr * hr - xi * hi)
        dhi[:, LANES:], dlo[:, LANES:] = split(xr * hi + xi * hr)
        spec[...] = dot(dhi[...], mid[2]) + dot(dhi[...], mid[3]) + dot(dlo[...], mid[2])
        cols = []
        for c in range(OWN):
            at = pl.ds(c * k1, k1)
            real, imag = spec[at, :LANES], spec[at, LANES:]
            cols.append(
                jnp.concatenate([real * twist[0] + imag * twist[1], imag * twist[0] - real * twist[1]], axis=0)
            )
        high, low = split(jnp.concatenate(cols, axis=1))
        signal = dot(last[0], high) + dot(last[1], high) + dot(last[0], low)
        for c in range(OWN):
            line[pl.ds(c, k1, stride=OWN), :] = signal[:, c * LANES : (c + 1) * LANES]

    for copy in local[1:6]:
        copy.wait()
    hsend[...] = to_parts(filt[...])
    exchange(hsend, hrecv, h_sem)
    for copy in local[6:] + local[:1]:
        copy.wait()
    top = 8

    def project(block, first_one=False):
        part = xg[block]
        at = pl.ds(pl.multiple_of(block * feats, feats), feats)
        for s in range(3):
            cols = pl.ds(s * chans, chans)
            term = dot(part, w[s, at, :])
            proj[top:, cols] = term if first_one else proj[top:, cols] + term

    project(own, True)
    x_first()
    for block in (own2, minus, plus):
        project(block)

    whole(hsend, h_sem.at[1]).wait()
    line[...] = hrecv[...].reshape(line.shape)
    forward(hspec, False)
    x_second()
    for block, waits in ((two, (0, 1)), (minus2, (1,)), (plus2, (0,)), (two2, (0, 1))):
        for h in waits:
            x_pull(block, h)
        project(block)
    halo = pltpu.make_async_remote_copy(
        src_ref=proj.at[pl.ds(rows, top)], dst_ref=proj.at[pl.ds(0, top)],
        send_sem=halo_sem.at[0], recv_sem=halo_sem.at[1],
        device_id={"ctx": (ctx + 1) % nctx}, device_id_type=MESH,
    )
    halo.start()
    halo.wait()
    proj[:top] = jnp.where(ctx == 0, 0.0, proj[:top])

    def stream(s):
        cols = pl.ds(s * chans, chans)
        return (
            taps[0, s : s + 1, :] * proj[top:, cols]
            + taps[1, s : s + 1, :] * proj[pl.ds(top - 1, rows), cols]
            + taps[2, s : s + 1, :] * proj[pl.ds(top - 2, rows), cols]
        )

    gated[...] = stream(0) * stream(2)
    gsend[...] = to_parts(gated[...]).astype(BF16)
    exchange(gsend, grecv, g_sem)
    gate[...] = stream(1)
    whole(gsend, g_sem.at[1]).wait()

    line[...] = grecv[...].astype(F32).reshape(line.shape)
    forward(spec, True)
    backward()
    csend[...] = line[...].reshape(csend.shape).astype(BF16)
    exchange(csend, crecv, c_sem)
    whole(csend, c_sem.at[1]).wait()
    back = crecv[...].astype(F32)
    for part in range(2):
        at = pl.ds(part * LANES, LANES)
        conv = back[:, part * OWN : (part + 1) * OWN, :].reshape(chans, LANES).T
        mixed = gate[at, :] * (conv + skip[...] * gated[at, :])
        yg[own, at, :] = mixed.astype(BF16)

    y_begin, y_first, y_second, y_pull, y_finish = gather(yg.at[own], yg, y_send, y_recv)

    def mix(block):
        at = pl.ds(pl.multiple_of(block * chans, chans), chans)
        return dot(yg[block], wo[at, :])

    y_begin()
    acc[...] = mix(own)
    y_first()
    for block in (own2, minus, plus):
        acc[...] += mix(block)
    y_second()
    for block, waits in ((two, (0, 1)), (minus2, (1,)), (plus2, (0,)), (two2, (0, 1))):
        for h in waits:
            y_pull(block, h)
        acc[...] += mix(block)
    out_ref[...] = acc[...].astype(BF16)

    x_finish()
    y_finish()
    whole(hsend, h_sem.at[0]).wait()
    whole(gsend, g_sem.at[0]).wait()
    whole(csend, c_sem.at[0]).wait()


def shards(nctx, nch, inputs, in_weight, short_kernel, long_filter, skip_gain, out_weight):
    rows, feats = inputs.shape
    width, _, chans = in_weight.shape
    mixed = out_weight.shape[1]
    length = rows * nctx
    consts = [jnp.asarray(t) for t in tables(length)]
    k1 = length // LANES
    operands = [
        inputs, jnp.transpose(in_weight, (1, 0, 2)), short_kernel, long_filter,
        skip_gain.reshape(1, chans), out_weight, *consts,
    ]
    vm = pltpu.VMEM
    parts = (nctx, 2 * OWN, LANES)
    scratch = [
        vm((nch, rows, feats), BF16), vm((3, width, chans), BF16), vm(short_kernel.shape, F32),
        vm((rows, chans), F32), vm((1, chans), F32), vm(out_weight.shape, BF16),
        *[vm(c.shape, c.dtype) for c in consts],
        vm((rows + 8, 3 * chans), F32), vm((rows, chans), F32), vm((rows, chans), F32),
        vm(parts, F32), vm(parts, F32), vm(parts, BF16), vm(parts, BF16), vm(parts, BF16), vm(parts, BF16),
        vm((nch, rows, chans), BF16),
        vm((k1 * OWN, LANES), F32), vm((k1 * OWN, 2 * LANES), F32), vm((k1 * OWN, 2 * LANES), F32),
        vm((k1 * OWN, 2 * LANES), BF16), vm((k1 * OWN, 2 * LANES), BF16), vm((rows, mixed), F32),
    ]
    dma = pltpu.SemaphoreType.DMA
    sems = [
        dma((10,)), dma((14,)), dma((nch, 2)), dma((2,)), dma((2,)), dma((2,)), dma((2,)), dma((14,)), dma((nch, 2)),
    ]
    return pl.pallas_call(
        functools.partial(kernel, nctx, nch, 2),
        out_shape=jax.ShapeDtypeStruct((rows, mixed), BF16),
        in_specs=[pl.BlockSpec(memory_space=pltpu.HBM)] * len(operands),
        out_specs=pl.BlockSpec(memory_space=pltpu.VMEM),
        scratch_shapes=scratch + sems,
        compiler_params=pltpu.CompilerParams(
            collective_id=0, has_side_effects=True, vmem_limit_bytes=40 * 1024 * 1024
        ),
    )(*operands)


def solution(mesh):
    placed = (
        P("ctx", "ch"),
        P(None, None, "ch"),
        P(None, None, "ch"),
        P("ctx", "ch"),
        P("ch"),
        P(None, "ch"),
    )
    body = functools.partial(shards, mesh.shape["ctx"], mesh.shape["ch"])
    return jax.shard_map(body, mesh=mesh, in_specs=placed, out_specs=P("ctx", "ch"), check_vma=False)
```

```python
import functools
import math

import jax
import jax.numpy as jnp
import ml_dtypes
import numpy as np
from jax import lax
from jax.experimental import pallas as pl
from jax.experimental.pallas import tpu as pltpu
from jax.sharding import PartitionSpec as P

MESH = pl.DeviceIdType.MESH
BF16 = jnp.bfloat16
F32 = jnp.float32
LANES = 128
OWN = 8


def halves(table):
    high = table.astype(ml_dtypes.bfloat16)
    low = (table - high.astype(np.float64)).astype(ml_dtypes.bfloat16)
    return np.stack([high, low])


def tables(length):
    rows = length // LANES
    k1 = np.arange(rows)[:, None] + 0.5
    n1 = np.arange(rows)[None, :]
    n2 = np.arange(LANES)[None, :]
    k2 = np.arange(LANES)[:, None]
    outer = 2.0 * math.pi * k1 * n1 / (2 * rows)
    first = np.concatenate([np.cos(outer), -np.sin(outer)], 0)
    turn = 2.0 * math.pi * k1 * n2 / (2 * length)
    twist = np.stack([np.cos(turn), -np.sin(turn)]).astype(np.float32)
    inner = 2.0 * math.pi * k2 * n2 / LANES
    cosine, sine = np.cos(inner), np.sin(inner)
    second = np.block([[cosine, -sine], [sine, cosine]])
    back = np.block([[cosine, sine], [-sine, cosine]])
    return (
        halves(first),
        halves(first.T / length),
        np.concatenate([halves(second), halves(back)]),
        twist,
    )


def ctx_order(count):
    size = (2, count // 4, 2) if count >= 4 else (1, 1, count)
    nz = size[1]
    far = sorted(range(nz), key=lambda z: -min(z, nz - z))
    every = [(y, z, c) for z in far for y in reversed(range(size[0])) for c in reversed(range(size[2]))]
    return size, [offset for offset in every if offset != (0, 0, 0)]


def split(value):
    high = value.astype(BF16)
    return high, (value - high.astype(F32)).astype(BF16)


def dot(left, right):
    return jnp.dot(left, right, preferred_element_type=F32)


def kernel(nctx, nch, ny, *refs):
    (
        x_hbm, w_hbm, taps_hbm, filt_hbm, skip_hbm, wo_hbm,
        first_hbm, last_hbm, mid_hbm, twist_hbm,
        out_ref,
        xg, w, taps, filt, skip, wo, first, last, mid, twist,
        proj, gate, gated, hsend, hrecv, gsend, grecv, csend, crecv, yg,
        line, spec, hspec, dhi, dlo, acc, tail_out, tails, tail_x,
        local_sem, x_send, x_recv, halo_sem, tail_sem, h_sem, g_sem, c_sem, y_send, y_recv,
    ) = refs
    ctx = lax.axis_index("ctx")
    ch = lax.axis_index("ch")
    rows, feats = x_hbm.shape
    chans = filt_hbm.shape[1]
    k1 = first_hbm.shape[2]

    nx = nch // ny
    half = rows // 2

    def at_ch(dx, dy):
        return ((ch // ny + dx) % nx) * ny + (ch % ny + dy) % ny

    own, plus, minus, two = at_ch(0, 0), at_ch(1, 0), at_ch(nx - 1, 0), at_ch(2, 0)
    own2, plus2, minus2, two2 = at_ch(0, 1), at_ch(1, 1), at_ch(nx - 1, 1), at_ch(2, 1)

    size, offsets = ctx_order(nctx)

    def ctx_peer(offset):
        low = ctx % size[2]
        z = (ctx // size[2]) % size[1]
        y = ctx // (size[1] * size[2])
        dy, dz, dc = offset
        return (((y + dy) % size[0]) * size[1] + (z + dz) % size[1]) * size[2] + (low + dc) % size[2]

    ctx_peers = [ctx_peer(offset) for offset in offsets]

    pairs = (
        (x_hbm, xg.at[own]), (filt_hbm, filt), (first_hbm, first), (mid_hbm, mid), (twist_hbm, twist),
        (w_hbm, w), (last_hbm, last), (taps_hbm, taps), (skip_hbm, skip), (wo_hbm, wo),
    )
    local = [pltpu.make_async_copy(s, d, local_sem.at[i]) for i, (s, d) in enumerate(pairs)]
    barrier = pltpu.get_barrier_semaphore()
    for step in range(1, nch):
        pl.semaphore_signal(barrier, inc=1, device_id={"ch": (ch + step) % nch}, device_id_type=MESH)
    for to in ctx_peers:
        pl.semaphore_signal(barrier, inc=1, device_id={"ctx": to}, device_id_type=MESH)
    for copy in local:
        copy.start()

    def to_parts(block):
        turned = block.T.reshape(nctx, OWN, rows)
        return jnp.concatenate([turned[:, :, :LANES], turned[:, :, LANES:]], axis=1)

    for copy in local[:2]:
        copy.wait()
    hsend[...] = to_parts(filt[...])
    tiles = feats // LANES
    last_rows = xg[own, pl.ds(rows - 16, 16), :].astype(F32)
    for r in range(2):
        for part in range(tiles):
            tail_out[pl.ds(r * tiles + part, 1), :] = last_rows[14 + r : 15 + r, part * LANES : (part + 1) * LANES]
    pl.semaphore_wait(barrier, nctx + nch - 2)


    def gather(source, slots, send, recv):
        started = []

        def piece(block, h):
            return slots.at[block, pl.ds(h * half, half)]

        def push(block, h, to, src=None):
            copy = pltpu.make_async_remote_copy(
                src_ref=piece(block, h) if src is None else src.at[pl.ds(h * half, half)],
                dst_ref=piece(block, h), send_sem=send.at[len(started)], recv_sem=recv.at[block, h],
                device_id={"ch": to}, device_id_type=MESH,
            )
            copy.start()
            started.append(copy)

        def pull(block, h):
            pltpu.make_async_remote_copy(
                src_ref=piece(block, h), dst_ref=piece(block, h), send_sem=send.at[0], recv_sem=recv.at[block, h],
                device_id={"ch": own2}, device_id_type=MESH,
            ).wait_recv()

        def begin(order):
            for h, to in order:
                push(own, h, to, source)

        def forward_first():
            pull(own2, 0), push(own2, 0, plus)
            pull(own2, 1), push(own2, 1, minus)
            pull(minus, 0), push(minus, 0, plus)
            pull(plus, 1), push(plus, 1, minus)
            pull(minus, 1), push(minus, 1, own2)
            pull(plus, 0), push(plus, 0, own2)

        def forward_second():
            pull(minus2, 0), push(minus2, 0, plus)
            pull(plus2, 1), push(plus2, 1, minus)

        def finish():
            for copy in started:
                copy.wait_send()

        return begin, forward_first, forward_second, pull, finish

    x_begin, x_first, x_second, x_pull, x_finish = gather(x_hbm, xg, x_send, x_recv)
    x_begin(((0, own2), (0, plus), (1, minus), (1, own2), (1, plus), (0, minus)))
    to_next = pltpu.make_async_remote_copy(
        src_ref=tail_out, dst_ref=tails.at[own], send_sem=halo_sem.at[0], recv_sem=halo_sem.at[1],
        device_id={"ctx": (ctx + 1) % nctx}, device_id_type=MESH,
    )
    to_next.start()


    def exchange(send, recv, sem):
        for to in ctx_peers:
            pltpu.make_async_remote_copy(
                src_ref=send.at[to], dst_ref=recv.at[ctx], send_sem=sem.at[0], recv_sem=sem.at[1],
                device_id={"ctx": to}, device_id_type=MESH,
            ).start()
        recv[pl.ds(ctx, 1)] = send[pl.ds(ctx, 1)]

    def whole(send, sem):
        part = send.at[pl.ds(0, nctx - 1)]
        return pltpu.make_async_copy(part, part, sem)

    def forward(result, exact):
        block = jnp.concatenate([line[pl.ds(c, k1, stride=OWN), :] for c in range(OWN)], axis=1)
        high, low = split(block)
        turned = dot(first[0], high) + dot(first[1], high)
        if not exact:
            turned = turned + dot(first[0], low)
        for c in range(OWN):
            real = turned[:k1, c * LANES : (c + 1) * LANES]
            imag = turned[k1:, c * LANES : (c + 1) * LANES]
            at = pl.ds(c * k1, k1)
            dhi[at, :LANES], dlo[at, :LANES] = split(real * twist[0] - imag * twist[1])
            dhi[at, LANES:], dlo[at, LANES:] = split(real * twist[1] + imag * twist[0])
        result[...] = dot(dhi[...], mid[0]) + dot(dhi[...], mid[1]) + dot(dlo[...], mid[0])

    def backward():
        xr, xi = spec[:, :LANES], spec[:, LANES:]
        hr, hi = hspec[:, :LANES], hspec[:, LANES:]
        dhi[:, :LANES], dlo[:, :LANES] = split(xr * hr - xi * hi)
        dhi[:, LANES:], dlo[:, LANES:] = split(xr * hi + xi * hr)
        spec[...] = dot(dhi[...], mid[2]) + dot(dhi[...], mid[3]) + dot(dlo[...], mid[2])
        cols = []
        for c in range(OWN):
            at = pl.ds(c * k1, k1)
            real, imag = spec[at, :LANES], spec[at, LANES:]
            cols.append(
                jnp.concatenate([real * twist[0] + imag * twist[1], imag * twist[0] - real * twist[1]], axis=0)
            )
        high, low = split(jnp.concatenate(cols, axis=1))
        signal = dot(last[0], high) + dot(last[1], high) + dot(last[0], low)
        for c in range(OWN):
            line[pl.ds(c, k1, stride=OWN), :] = signal[:, c * LANES : (c + 1) * LANES]

    exchange(hsend, hrecv, h_sem)
    top = 8

    def project(block, first_one=False):
        part = xg[block]
        at = pl.ds(pl.multiple_of(block * feats, feats), feats)
        for s in range(3):
            cols = pl.ds(s * chans, chans)
            term = dot(part, w[s, at, :])
            proj[top:, cols] = term if first_one else proj[top:, cols] + term

    to_next.wait_recv()
    to_ch = [
        pltpu.make_async_remote_copy(
            src_ref=tails.at[own], dst_ref=tails.at[own], send_sem=tail_sem.at[0], recv_sem=tail_sem.at[1],
            device_id={"ch": (ch + step) % nch}, device_id_type=MESH,
        )
        for step in range(1, nch)
    ]
    for copy in to_ch:
        copy.start()
    x_first()
    for copy in local[2:]:
        copy.wait()
    project(own, True)
    for block in (own2, minus, plus):
        project(block)

    whole(hsend, h_sem.at[1]).wait()
    line[...] = hrecv[...].reshape(line.shape)
    forward(hspec, False)
    x_second()
    others = tails.at[pl.ds(0, nch - 1)]
    pltpu.make_async_copy(others, others, tail_sem.at[1]).wait()
    tail_x[...] = jnp.zeros_like(tail_x)
    for block in range(nch):
        for r in range(2):
            for part in range(tiles):
                at = pl.ds(block * feats + part * LANES, LANES)
                tail_x[pl.ds(top - 2 + r, 1), at] = tails[block, pl.ds(r * tiles + part, 1), :]
    for s in range(3):
        before = dot(tail_x[...].astype(BF16), w[s])
        proj[:top, pl.ds(s * chans, chans)] = jnp.where(ctx == 0, 0.0, before)
    for block, waits in ((two, (0, 1)), (minus2, (1,)), (plus2, (0,)), (two2, (0, 1))):
        for h in waits:
            x_pull(block, h)
        project(block)
    def stream(s):
        cols = pl.ds(s * chans, chans)
        return (
            taps[0, s : s + 1, :] * proj[top:, cols]
            + taps[1, s : s + 1, :] * proj[pl.ds(top - 1, rows), cols]
            + taps[2, s : s + 1, :] * proj[pl.ds(top - 2, rows), cols]
        )

    gated[...] = stream(0) * stream(2)
    gsend[...] = to_parts(gated[...]).astype(BF16)
    exchange(gsend, grecv, g_sem)
    gate[...] = stream(1)
    whole(gsend, g_sem.at[1]).wait()

    line[...] = grecv[...].astype(F32).reshape(line.shape)
    forward(spec, True)
    backward()
    csend[...] = line[...].reshape(csend.shape).astype(BF16)
    exchange(csend, crecv, c_sem)
    whole(csend, c_sem.at[1]).wait()
    y_begin, y_first, y_second, y_pull, y_finish = gather(yg.at[own], yg, y_send, y_recv)
    for part, order in ((0, (own2, plus, minus)), (1, (own2, minus, plus))):
        at = pl.ds(part * LANES, LANES)
        back = crecv[:, part * OWN : (part + 1) * OWN, :].astype(F32)
        conv = back.reshape(chans, LANES).T
        mixed = gate[at, :] * (conv + skip[...] * gated[at, :])
        yg[own, at, :] = mixed.astype(BF16)
        y_begin([(part, to) for to in order])

    def mix(block):
        at = pl.ds(pl.multiple_of(block * chans, chans), chans)
        return dot(yg[block], wo[at, :])

    acc[...] = mix(own)
    y_first()
    for block in (own2, minus, plus):
        acc[...] += mix(block)
    y_second()
    for block, waits in ((two, (0, 1)), (minus2, (1,)), (plus2, (0,)), (two2, (0, 1))):
        for h in waits:
            y_pull(block, h)
        acc[...] += mix(block)
    out_ref[...] = acc[...].astype(BF16)

    x_finish()
    y_finish()
    to_next.wait_send()
    pltpu.make_async_copy(others, others, tail_sem.at[0]).wait()
    whole(hsend, h_sem.at[0]).wait()
    whole(gsend, g_sem.at[0]).wait()
    whole(csend, c_sem.at[0]).wait()


def shards(nctx, nch, inputs, in_weight, short_kernel, long_filter, skip_gain, out_weight):
    rows, feats = inputs.shape
    width, _, chans = in_weight.shape
    mixed = out_weight.shape[1]
    length = rows * nctx
    consts = [jnp.asarray(t) for t in tables(length)]
    k1 = length // LANES
    operands = [
        inputs, jnp.transpose(in_weight, (1, 0, 2)), short_kernel, long_filter,
        skip_gain.reshape(1, chans), out_weight, *consts,
    ]
    vm = pltpu.VMEM
    parts = (nctx, 2 * OWN, LANES)
    scratch = [
        vm((nch, rows, feats), BF16), vm((3, width, chans), BF16), vm(short_kernel.shape, F32),
        vm((rows, chans), F32), vm((1, chans), F32), vm(out_weight.shape, BF16),
        *[vm(c.shape, c.dtype) for c in consts],
        vm((rows + 8, 3 * chans), F32), vm((rows, chans), F32), vm((rows, chans), F32),
        vm(parts, F32), vm(parts, F32), vm(parts, BF16), vm(parts, BF16), vm(parts, BF16), vm(parts, BF16),
        vm((nch, rows, chans), BF16),
        vm((k1 * OWN, LANES), F32), vm((k1 * OWN, 2 * LANES), F32), vm((k1 * OWN, 2 * LANES), F32),
        vm((k1 * OWN, 2 * LANES), BF16), vm((k1 * OWN, 2 * LANES), BF16), vm((rows, mixed), F32),
        vm((2 * feats // LANES, LANES), F32), vm((nch, 2 * feats // LANES, LANES), F32), vm((8, width), F32),
    ]
    dma = pltpu.SemaphoreType.DMA
    sems = [
        dma((10,)), dma((14,)), dma((nch, 2)), dma((2,)), dma((2,)), dma((2,)), dma((2,)), dma((2,)),
        dma((14,)), dma((nch, 2)),
    ]
    return pl.pallas_call(
        functools.partial(kernel, nctx, nch, 2),
        out_shape=jax.ShapeDtypeStruct((rows, mixed), BF16),
        in_specs=[pl.BlockSpec(memory_space=pltpu.HBM)] * len(operands),
        out_specs=pl.BlockSpec(memory_space=pltpu.VMEM),
        scratch_shapes=scratch + sems,
        compiler_params=pltpu.CompilerParams(
            collective_id=0, has_side_effects=True, vmem_limit_bytes=63 * 1024 * 1024
        ),
    )(*operands)


def solution(mesh):
    placed = (
        P("ctx", "ch"),
        P(None, None, "ch"),
        P(None, None, "ch"),
        P("ctx", "ch"),
        P("ch"),
        P(None, "ch"),
    )
    body = functools.partial(shards, mesh.shape["ctx"], mesh.shape["ch"])
    return jax.shard_map(body, mesh=mesh, in_specs=placed, out_specs=P("ctx", "ch"), check_vma=False)
```

```python
import functools
import math

import jax
import jax.numpy as jnp
import ml_dtypes
import numpy as np
from jax import lax
from jax.experimental import pallas as pl
from jax.experimental.pallas import tpu as pltpu
from jax.sharding import PartitionSpec as P

MESH = pl.DeviceIdType.MESH
BF16 = jnp.bfloat16
F32 = jnp.float32
LANES = 128
OWN = 8


def halves(table):
    high = table.astype(ml_dtypes.bfloat16)
    low = (table - high.astype(np.float64)).astype(ml_dtypes.bfloat16)
    return np.stack([high, low])


def tables(length):
    rows = length // LANES
    k1 = np.arange(rows)[:, None] + 0.5
    n1 = np.arange(rows)[None, :]
    n2 = np.arange(LANES)[None, :]
    k2 = np.arange(LANES)[:, None]
    outer = 2.0 * math.pi * k1 * n1 / (2 * rows)
    first = np.concatenate([np.cos(outer), -np.sin(outer)], 0)
    turn = 2.0 * math.pi * k1 * n2 / (2 * length)
    twist = np.stack([np.cos(turn), -np.sin(turn)]).astype(np.float32)
    inner = 2.0 * math.pi * k2 * n2 / LANES
    cosine, sine = np.cos(inner), np.sin(inner)
    second = np.block([[cosine, -sine], [sine, cosine]])
    back = np.block([[cosine, sine], [-sine, cosine]])
    return (
        halves(first),
        halves(first.T / length),
        np.concatenate([halves(second), halves(back)]),
        twist,
    )


def ctx_order(count):
    size = (2, count // 4, 2) if count >= 4 else (1, 1, count)
    nz = size[1]
    far = sorted(range(nz), key=lambda z: -min(z, nz - z))
    every = [(y, z, c) for z in far for y in reversed(range(size[0])) for c in reversed(range(size[2]))]
    return size, [offset for offset in every if offset != (0, 0, 0)]


def split(value):
    high = value.astype(BF16)
    return high, (value - high.astype(F32)).astype(BF16)


def dot(left, right):
    return jnp.dot(left, right, preferred_element_type=F32)


def kernel(nctx, nch, ny, *refs):
    (
        x_hbm, w_hbm, taps_hbm, filt_hbm, skip_hbm, wo_hbm,
        first_hbm, last_hbm, mid_hbm, twist_hbm,
        out_ref,
        xg, w, taps, filt, skip, wo, first, last, mid, twist,
        proj, gate, gated, hsend, hrecv, gsend, grecv, csend, crecv, yg,
        line, spec, hspec, dhi, dlo, acc, tail_out, tails, tail_x,
        heard, local_sem, x_send, x_recv, halo_sem, tail_sem, h_sem, g_sem, c_sem, y_send, y_recv,
    ) = refs
    ctx = lax.axis_index("ctx")
    ch = lax.axis_index("ch")
    rows, feats = x_hbm.shape
    chans = filt_hbm.shape[1]
    k1 = first_hbm.shape[2]

    nx = nch // ny
    half = rows // 2

    def at_ch(dx, dy):
        return ((ch // ny + dx) % nx) * ny + (ch % ny + dy) % ny

    own, plus, minus, two = at_ch(0, 0), at_ch(1, 0), at_ch(nx - 1, 0), at_ch(2, 0)
    own2, plus2, minus2, two2 = at_ch(0, 1), at_ch(1, 1), at_ch(nx - 1, 1), at_ch(2, 1)

    size, offsets = ctx_order(nctx)

    def ctx_peer(offset):
        low = ctx % size[2]
        z = (ctx // size[2]) % size[1]
        y = ctx // (size[1] * size[2])
        dy, dz, dc = offset
        return (((y + dy) % size[0]) * size[1] + (z + dz) % size[1]) * size[2] + (low + dc) % size[2]

    ctx_peers = [ctx_peer(offset) for offset in offsets]

    pairs = (
        (x_hbm, xg.at[own]), (filt_hbm, filt), (first_hbm, first), (mid_hbm, mid), (twist_hbm, twist),
        (w_hbm, w), (last_hbm, last), (taps_hbm, taps), (skip_hbm, skip), (wo_hbm, wo),
    )
    local = [pltpu.make_async_copy(s, d, local_sem.at[i]) for i, (s, d) in enumerate(pairs)]
    ways = [(0, 0, 1)] if size[2] > 1 else []
    z_ways = [(0, 1, 0), (0, size[1] - 1, 0)] if size[1] > 1 else []
    y_ways = [(1, 0, 0)] if size[0] > 1 else []
    barrier = pltpu.get_barrier_semaphore()

    def greet(sem, chs, offs):
        for to in chs:
            pl.semaphore_signal(sem, inc=1, device_id={"ch": to}, device_id_type=MESH)
        for offset in offs:
            pl.semaphore_signal(sem, inc=1, device_id={"ctx": ctx_peer(offset)}, device_id_type=MESH)

    near = (plus, minus, own2)
    rounds = [(near, ways), ((own2,), z_ways)] + [((), z_ways)] * 3

    def tell(i):
        greet(heard.at[i], *rounds[i])

    def hear(i):
        count = len(rounds[i][0]) + len(rounds[i][1])
        if count:
            pl.semaphore_wait(heard.at[i], count)

    greet(barrier, near, ways + y_ways + z_ways)
    for copy in local:
        copy.start()

    def to_parts(block):
        turned = block.T.reshape(nctx, OWN, rows)
        return jnp.concatenate([turned[:, :, :LANES], turned[:, :, LANES:]], axis=1)

    for copy in local[:2]:
        copy.wait()
    hsend[...] = to_parts(filt[...])
    tiles = feats // LANES
    last_rows = xg[own, pl.ds(rows - 16, 16), :].astype(F32)
    for r in range(2):
        for part in range(tiles):
            tail_out[pl.ds(r * tiles + part, 1), :] = last_rows[14 + r : 15 + r, part * LANES : (part + 1) * LANES]
    pl.semaphore_wait(barrier, len(near) + len(ways + y_ways + z_ways))


    def gather(source, slots, send, recv):
        started = []

        def piece(block, h):
            return slots.at[block, pl.ds(h * half, half)]

        def push(block, h, to, src=None):
            copy = pltpu.make_async_remote_copy(
                src_ref=piece(block, h) if src is None else src.at[pl.ds(h * half, half)],
                dst_ref=piece(block, h), send_sem=send.at[len(started)], recv_sem=recv.at[block, h],
                device_id={"ch": to}, device_id_type=MESH,
            )
            copy.start()
            started.append(copy)

        def pull(block, h):
            pltpu.make_async_remote_copy(
                src_ref=piece(block, h), dst_ref=piece(block, h), send_sem=send.at[0], recv_sem=recv.at[block, h],
                device_id={"ch": own2}, device_id_type=MESH,
            ).wait_recv()

        def begin(order):
            for h, to in order:
                push(own, h, to, source)

        def forward_own2():
            pull(own2, 0), push(own2, 0, plus)
            pull(own2, 1), push(own2, 1, minus)

        def forward_near():
            pull(minus, 0), push(minus, 0, plus)
            pull(plus, 1), push(plus, 1, minus)

        def cross():
            pull(minus, 1), push(minus, 1, own2)
            pull(plus, 0), push(plus, 0, own2)

        def forward_second():
            pull(minus2, 0), push(minus2, 0, plus)
            pull(plus2, 1), push(plus2, 1, minus)

        def finish():
            for copy in started:
                copy.wait_send()

        return begin, (forward_own2, forward_near, cross), forward_second, pull, finish

    x_begin, x_first, x_second, x_pull, x_finish = gather(x_hbm, xg, x_send, x_recv)
    x_begin(((0, own2), (0, plus), (1, minus), (1, own2), (1, plus), (0, minus)))
    to_next = pltpu.make_async_remote_copy(
        src_ref=tail_out, dst_ref=tails.at[own], send_sem=halo_sem.at[0], recv_sem=halo_sem.at[1],
        device_id={"ctx": (ctx + 1) % nctx}, device_id_type=MESH,
    )
    tell(0)
    hear(0)
    tell(1)
    hear(1)
    tell(2)
    to_next.start()


    def exchange(send, recv, sem):
        for to in ctx_peers:
            pltpu.make_async_remote_copy(
                src_ref=send.at[to], dst_ref=recv.at[ctx], send_sem=sem.at[0], recv_sem=sem.at[1],
                device_id={"ctx": to}, device_id_type=MESH,
            ).start()
        recv[pl.ds(ctx, 1)] = send[pl.ds(ctx, 1)]

    def whole(send, sem):
        part = send.at[pl.ds(0, nctx - 1)]
        return pltpu.make_async_copy(part, part, sem)

    def forward(result, exact):
        block = jnp.concatenate([line[pl.ds(c, k1, stride=OWN), :] for c in range(OWN)], axis=1)
        high, low = split(block)
        turned = dot(first[0], high) + dot(first[1], high)
        if not exact:
            turned = turned + dot(first[0], low)
        for c in range(OWN):
            real = turned[:k1, c * LANES : (c + 1) * LANES]
            imag = turned[k1:, c * LANES : (c + 1) * LANES]
            at = pl.ds(c * k1, k1)
            dhi[at, :LANES], dlo[at, :LANES] = split(real * twist[0] - imag * twist[1])
            dhi[at, LANES:], dlo[at, LANES:] = split(real * twist[1] + imag * twist[0])
        result[...] = dot(dhi[...], mid[0]) + dot(dhi[...], mid[1]) + dot(dlo[...], mid[0])

    def backward():
        xr, xi = spec[:, :LANES], spec[:, LANES:]
        hr, hi = hspec[:, :LANES], hspec[:, LANES:]
        dhi[:, :LANES], dlo[:, :LANES] = split(xr * hr - xi * hi)
        dhi[:, LANES:], dlo[:, LANES:] = split(xr * hi + xi * hr)
        spec[...] = dot(dhi[...], mid[2]) + dot(dhi[...], mid[3]) + dot(dlo[...], mid[2])
        cols = []
        for c in range(OWN):
            at = pl.ds(c * k1, k1)
            real, imag = spec[at, :LANES], spec[at, LANES:]
            cols.append(
                jnp.concatenate([real * twist[0] + imag * twist[1], imag * twist[0] - real * twist[1]], axis=0)
            )
        high, low = split(jnp.concatenate(cols, axis=1))
        signal = dot(last[0], high) + dot(last[1], high) + dot(last[0], low)
        for c in range(OWN):
            line[pl.ds(c, k1, stride=OWN), :] = signal[:, c * LANES : (c + 1) * LANES]

    top = 8

    def project(block, first_one=False):
        part = xg[block]
        at = pl.ds(pl.multiple_of(block * feats, feats), feats)
        for s in range(3):
            cols = pl.ds(s * chans, chans)
            term = dot(part, w[s, at, :])
            proj[top:, cols] = term if first_one else proj[top:, cols] + term

    x_first[0]()
    hear(2)
    tell(3)
    x_first[1]()
    hear(3)
    tell(4)
    to_next.wait_recv()
    to_ch = [
        pltpu.make_async_remote_copy(
            src_ref=tails.at[own], dst_ref=tails.at[own], send_sem=tail_sem.at[0], recv_sem=tail_sem.at[1],
            device_id={"ch": (ch + step) % nch}, device_id_type=MESH,
        )
        for step in range(1, nch)
    ]
    for copy in to_ch:
        copy.start()
    x_first[2]()
    hear(4)
    for copy in local[2:]:
        copy.wait()
    project(own, True)
    for block in (own2, minus, plus):
        project(block)

    x_second()
    exchange(hsend, hrecv, h_sem)
    others = tails.at[pl.ds(0, nch - 1)]
    pltpu.make_async_copy(others, others, tail_sem.at[1]).wait()
    tail_x[...] = jnp.zeros_like(tail_x)
    for block in range(nch):
        for r in range(2):
            for part in range(tiles):
                at = pl.ds(block * feats + part * LANES, LANES)
                tail_x[pl.ds(top - 2 + r, 1), at] = tails[block, pl.ds(r * tiles + part, 1), :]
    for s in range(3):
        before = dot(tail_x[...].astype(BF16), w[s])
        proj[:top, pl.ds(s * chans, chans)] = jnp.where(ctx == 0, 0.0, before)
    for block, waits in ((two, (0, 1)), (minus2, (1,)), (plus2, (0,)), (two2, (0, 1))):
        for h in waits:
            x_pull(block, h)
        project(block)
    def stream(s):
        cols = pl.ds(s * chans, chans)
        return (
            taps[0, s : s + 1, :] * proj[top:, cols]
            + taps[1, s : s + 1, :] * proj[pl.ds(top - 1, rows), cols]
            + taps[2, s : s + 1, :] * proj[pl.ds(top - 2, rows), cols]
        )

    gated[...] = stream(0) * stream(2)
    gsend[...] = to_parts(gated[...]).astype(BF16)
    exchange(gsend, grecv, g_sem)
    gate[...] = stream(1)
    whole(hsend, h_sem.at[1]).wait()
    line[...] = hrecv[...].reshape(line.shape)
    forward(hspec, False)
    whole(gsend, g_sem.at[1]).wait()

    line[...] = grecv[...].astype(F32).reshape(line.shape)
    forward(spec, True)
    backward()
    csend[...] = line[...].reshape(csend.shape).astype(BF16)
    exchange(csend, crecv, c_sem)
    whole(csend, c_sem.at[1]).wait()
    y_begin, y_first, y_second, y_pull, y_finish = gather(yg.at[own], yg, y_send, y_recv)
    for part, order in ((0, (own2, plus, minus)), (1, (own2, minus, plus))):
        at = pl.ds(part * LANES, LANES)
        back = crecv[:, part * OWN : (part + 1) * OWN, :].astype(F32)
        conv = back.reshape(chans, LANES).T
        mixed = gate[at, :] * (conv + skip[...] * gated[at, :])
        yg[own, at, :] = mixed.astype(BF16)
        y_begin([(part, to) for to in order])

    def mix(block):
        at = pl.ds(pl.multiple_of(block * chans, chans), chans)
        return dot(yg[block], wo[at, :])

    acc[...] = mix(own)
    for forward_part in y_first:
        forward_part()
    for block in (own2, minus, plus):
        acc[...] += mix(block)
    y_second()
    for block, waits in ((two, (0, 1)), (minus2, (1,)), (plus2, (0,)), (two2, (0, 1))):
        for h in waits:
            y_pull(block, h)
        acc[...] += mix(block)
    out_ref[...] = acc[...].astype(BF16)

    x_finish()
    y_finish()
    to_next.wait_send()
    pltpu.make_async_copy(others, others, tail_sem.at[0]).wait()
    whole(hsend, h_sem.at[0]).wait()
    whole(gsend, g_sem.at[0]).wait()
    whole(csend, c_sem.at[0]).wait()


def shards(nctx, nch, inputs, in_weight, short_kernel, long_filter, skip_gain, out_weight):
    rows, feats = inputs.shape
    width, _, chans = in_weight.shape
    mixed = out_weight.shape[1]
    length = rows * nctx
    consts = [jnp.asarray(t) for t in tables(length)]
    k1 = length // LANES
    operands = [
        inputs, jnp.transpose(in_weight, (1, 0, 2)), short_kernel, long_filter,
        skip_gain.reshape(1, chans), out_weight, *consts,
    ]
    vm = pltpu.VMEM
    parts = (nctx, 2 * OWN, LANES)
    scratch = [
        vm((nch, rows, feats), BF16), vm((3, width, chans), BF16), vm(short_kernel.shape, F32),
        vm((rows, chans), F32), vm((1, chans), F32), vm(out_weight.shape, BF16),
        *[vm(c.shape, c.dtype) for c in consts],
        vm((rows + 8, 3 * chans), F32), vm((rows, chans), F32), vm((rows, chans), F32),
        vm(parts, F32), vm(parts, F32), vm(parts, BF16), vm(parts, BF16), vm(parts, BF16), vm(parts, BF16),
        vm((nch, rows, chans), BF16),
        vm((k1 * OWN, LANES), F32), vm((k1 * OWN, 2 * LANES), F32), vm((k1 * OWN, 2 * LANES), F32),
        vm((k1 * OWN, 2 * LANES), BF16), vm((k1 * OWN, 2 * LANES), BF16), vm((rows, mixed), F32),
        vm((2 * feats // LANES, LANES), F32), vm((nch, 2 * feats // LANES, LANES), F32), vm((8, width), F32),
    ]
    dma = pltpu.SemaphoreType.DMA
    sems = [
        pltpu.SemaphoreType.REGULAR((5,)), dma((10,)), dma((14,)), dma((nch, 2)), dma((2,)), dma((2,)), dma((2,)), dma((2,)), dma((2,)),
        dma((14,)), dma((nch, 2)),
    ]
    return pl.pallas_call(
        functools.partial(kernel, nctx, nch, 2),
        out_shape=pltpu.VMEM((rows, mixed), BF16),
        in_specs=[pl.BlockSpec(memory_space=pltpu.HBM)] * len(operands),
        out_specs=pl.BlockSpec(memory_space=pltpu.VMEM),
        scratch_shapes=scratch + sems,
        compiler_params=pltpu.CompilerParams(
            collective_id=0, has_side_effects=True, vmem_limit_bytes=60 * 1024 * 1024
        ),
    )(*[pltpu.with_memory_space_constraint(o, pltpu.HBM) for o in operands])


def solution(mesh):
    placed = (
        P("ctx", "ch"),
        P(None, None, "ch"),
        P(None, None, "ch"),
        P("ctx", "ch"),
        P("ch"),
        P(None, "ch"),
    )
    body = functools.partial(shards, mesh.shape["ctx"], mesh.shape["ch"])
    return jax.shard_map(body, mesh=mesh, in_specs=placed, out_specs=P("ctx", "ch"), check_vma=False)
```

```python
import functools
import math

import jax
import jax.numpy as jnp
import ml_dtypes
import numpy as np
from jax import lax
from jax.experimental import pallas as pl
from jax.experimental.pallas import tpu as pltpu
from jax.sharding import PartitionSpec as P

MESH = pl.DeviceIdType.MESH
BF16 = jnp.bfloat16
F32 = jnp.float32
LANES = 128
OWN = 8


def halves(table):
    high = table.astype(ml_dtypes.bfloat16)
    low = (table - high.astype(np.float64)).astype(ml_dtypes.bfloat16)
    return np.stack([high, low])


def tables(length):
    rows = length // LANES
    k1 = np.arange(rows)[:, None] + 0.5
    n1 = np.arange(rows)[None, :]
    n2 = np.arange(LANES)[None, :]
    k2 = np.arange(LANES)[:, None]
    outer = 2.0 * math.pi * k1 * n1 / (2 * rows)
    first = np.concatenate([np.cos(outer), -np.sin(outer)], 0)
    turn = 2.0 * math.pi * k1 * n2 / (2 * length)
    twist = np.stack([np.cos(turn), -np.sin(turn)]).astype(np.float32)
    inner = 2.0 * math.pi * k2 * n2 / LANES
    cosine, sine = np.cos(inner), np.sin(inner)
    second = np.block([[cosine, -sine], [sine, cosine]])
    back = np.block([[cosine, sine], [-sine, cosine]])
    return (
        halves(first),
        halves(first.T / length),
        np.concatenate([halves(second), halves(back)]),
        twist,
    )


def ctx_order(count):
    size = (2, count // 4, 2) if count >= 4 else (1, 1, count)
    nz = size[1]
    far = sorted(range(nz), key=lambda z: -min(z, nz - z))
    every = [(y, z, c) for z in far for y in reversed(range(size[0])) for c in reversed(range(size[2]))]
    return size, [offset for offset in every if offset != (0, 0, 0)]


def split(value):
    high = value.astype(BF16)
    return high, (value - high.astype(F32)).astype(BF16)


def dot(left, right):
    return jnp.dot(left, right, preferred_element_type=F32)


def kernel(nctx, nch, ny, *refs):
    (
        x_hbm, w_hbm, taps_hbm, filt_hbm, skip_hbm, wo_hbm,
        first_hbm, last_hbm, mid_hbm, twist_hbm,
        out_ref,
        xg, w, taps, filt, skip, wo, first, last, mid, twist,
        proj, gate, gated, hsend, hrecv, gsend, grecv, csend, crecv, yg,
        line, spec, hspec, dhi, dlo, acc, tail_out, tails, tail_x,
        heard, local_sem, x_send, x_recv, halo_sem, tail_sem, h_sem, g_sem, c_sem, y_send, y_recv,
    ) = refs
    ctx = lax.axis_index("ctx")
    ch = lax.axis_index("ch")
    rows, feats = x_hbm.shape
    chans = filt_hbm.shape[1]
    k1 = first_hbm.shape[2]

    nx = nch // ny
    half = rows // 2

    def at_ch(dx, dy):
        return ((ch // ny + dx) % nx) * ny + (ch % ny + dy) % ny

    own, plus, minus, two = at_ch(0, 0), at_ch(1, 0), at_ch(nx - 1, 0), at_ch(2, 0)
    own2, plus2, minus2, two2 = at_ch(0, 1), at_ch(1, 1), at_ch(nx - 1, 1), at_ch(2, 1)

    size, offsets = ctx_order(nctx)

    def ctx_peer(offset):
        low = ctx % size[2]
        z = (ctx // size[2]) % size[1]
        y = ctx // (size[1] * size[2])
        dy, dz, dc = offset
        return (((y + dy) % size[0]) * size[1] + (z + dz) % size[1]) * size[2] + (low + dc) % size[2]

    ctx_peers = [ctx_peer(offset) for offset in offsets]

    pairs = (
        (x_hbm, xg.at[own]), (filt_hbm, filt), (first_hbm, first), (mid_hbm, mid), (twist_hbm, twist),
        (w_hbm, w), (last_hbm, last), (taps_hbm, taps), (skip_hbm, skip), (wo_hbm, wo),
    )
    local = [pltpu.make_async_copy(s, d, local_sem.at[i]) for i, (s, d) in enumerate(pairs)]
    ways = [(0, 0, 1)] if size[2] > 1 else []
    z_ways = [(0, 1, 0), (0, size[1] - 1, 0)] if size[1] > 1 else []
    y_ways = [(1, 0, 0)] if size[0] > 1 else []
    barrier = pltpu.get_barrier_semaphore()

    def greet(sem, chs, offs):
        for to in chs:
            pl.semaphore_signal(sem, inc=1, device_id={"ch": to}, device_id_type=MESH)
        for offset in offs:
            pl.semaphore_signal(sem, inc=1, device_id={"ctx": ctx_peer(offset)}, device_id_type=MESH)

    near = (plus, minus, own2)
    rounds = [(near, ways), ((own2,), z_ways)] + [((), z_ways)] * 3

    def tell(i):
        greet(heard.at[i], *rounds[i])

    def hear(i):
        count = len(rounds[i][0]) + len(rounds[i][1])
        if count:
            pl.semaphore_wait(heard.at[i], count)

    greet(barrier, near, ways + y_ways + z_ways)
    for copy in local:
        copy.start()

    def to_parts(block):
        turned = block.T.reshape(nctx, OWN, rows)
        return jnp.concatenate([turned[:, :, :LANES], turned[:, :, LANES:]], axis=1)

    pl.semaphore_wait(barrier, len(near) + len(ways + y_ways + z_ways))


    core = ctx % size[2]

    def on(only, act):
        if only is None:
            act()
        else:
            pl.when(core == only)(act)

    def gather(source, slots, send, recv):
        started = []

        def piece(block, h):
            return slots.at[block, pl.ds(h * half, half)]

        def push(block, h, to, src=None, only=None):
            copy = pltpu.make_async_remote_copy(
                src_ref=piece(block, h) if src is None else src.at[pl.ds(h * half, half)],
                dst_ref=piece(block, h), send_sem=send.at[len(started)], recv_sem=recv.at[block, h],
                device_id={"ch": to}, device_id_type=MESH,
            )
            on(only, copy.start)
            started.append((only, copy))

        def pull(block, h, only=None):
            copy = pltpu.make_async_remote_copy(
                src_ref=piece(block, h), dst_ref=piece(block, h), send_sem=send.at[0], recv_sem=recv.at[block, h],
                device_id={"ch": own2}, device_id_type=MESH,
            )
            on(only, copy.wait_recv)

        def finish():
            for only, copy in started:
                on(only, copy.wait_send)

        return push, pull, finish

    x_push, x_pull, x_finish = gather(x_hbm, xg, x_send, x_recv)
    for h, to in ((0, own2), (0, plus), (1, minus), (1, own2), (1, plus), (0, minus)):
        x_push(own, h, to, x_hbm)
    to_next = pltpu.make_async_remote_copy(
        src_ref=tail_out, dst_ref=tails.at[own], send_sem=halo_sem.at[0], recv_sem=halo_sem.at[1],
        device_id={"ctx": (ctx + 1) % nctx}, device_id_type=MESH,
    )
    tell(0)
    for copy in local[:2]:
        copy.wait()
    hsend[...] = to_parts(filt[...])
    tiles = feats // LANES
    last_rows = xg[own, pl.ds(rows - 16, 16), :].astype(F32)
    for r in range(2):
        for part in range(tiles):
            tail_out[pl.ds(r * tiles + part, 1), :] = last_rows[14 + r : 15 + r, part * LANES : (part + 1) * LANES]
    hear(0)
    tell(1)
    hear(1)
    tell(2)
    to_next.start()


    def exchange(send, recv, sem):
        for to in ctx_peers:
            pltpu.make_async_remote_copy(
                src_ref=send.at[to], dst_ref=recv.at[ctx], send_sem=sem.at[0], recv_sem=sem.at[1],
                device_id={"ctx": to}, device_id_type=MESH,
            ).start()
        recv[pl.ds(ctx, 1)] = send[pl.ds(ctx, 1)]

    def whole(send, sem):
        part = send.at[pl.ds(0, nctx - 1)]
        return pltpu.make_async_copy(part, part, sem)

    def forward(result, exact):
        block = jnp.concatenate([line[pl.ds(c, k1, stride=OWN), :] for c in range(OWN)], axis=1)
        high, low = split(block)
        turned = dot(first[0], high) + dot(first[1], high)
        if not exact:
            turned = turned + dot(first[0], low)
        for c in range(OWN):
            real = turned[:k1, c * LANES : (c + 1) * LANES]
            imag = turned[k1:, c * LANES : (c + 1) * LANES]
            at = pl.ds(c * k1, k1)
            dhi[at, :LANES], dlo[at, :LANES] = split(real * twist[0] - imag * twist[1])
            dhi[at, LANES:], dlo[at, LANES:] = split(real * twist[1] + imag * twist[0])
        result[...] = dot(dhi[...], mid[0]) + dot(dhi[...], mid[1]) + dot(dlo[...], mid[0])

    def backward():
        xr, xi = spec[:, :LANES], spec[:, LANES:]
        hr, hi = hspec[:, :LANES], hspec[:, LANES:]
        dhi[:, :LANES], dlo[:, :LANES] = split(xr * hr - xi * hi)
        dhi[:, LANES:], dlo[:, LANES:] = split(xr * hi + xi * hr)
        spec[...] = dot(dhi[...], mid[2]) + dot(dhi[...], mid[3]) + dot(dlo[...], mid[2])
        cols = []
        for c in range(OWN):
            at = pl.ds(c * k1, k1)
            real, imag = spec[at, :LANES], spec[at, LANES:]
            cols.append(
                jnp.concatenate([real * twist[0] + imag * twist[1], imag * twist[0] - real * twist[1]], axis=0)
            )
        high, low = split(jnp.concatenate(cols, axis=1))
        signal = dot(last[0], high) + dot(last[1], high) + dot(last[0], low)
        for c in range(OWN):
            line[pl.ds(c, k1, stride=OWN), :] = signal[:, c * LANES : (c + 1) * LANES]

    top = 8

    def project(block, first_one=False):
        part = xg[block]
        at = pl.ds(pl.multiple_of(block * feats, feats), feats)
        for s in range(3):
            cols = pl.ds(s * chans, chans)
            term = dot(part, w[s, at, :])
            proj[top:, cols] = term if first_one else proj[top:, cols] + term

    x_pull(minus, 0), x_push(minus, 0, plus)
    x_pull(plus, 1), x_push(plus, 1, minus)
    hear(2)
    tell(3)
    x_pull(own2, 0), x_push(own2, 0, plus), x_push(own2, 0, minus, only=0)
    x_pull(own2, 1), x_push(own2, 1, minus), x_push(own2, 1, plus, only=0)
    hear(3)
    tell(4)
    to_next.wait_recv()
    to_ch = [
        pltpu.make_async_remote_copy(
            src_ref=tails.at[own], dst_ref=tails.at[own], send_sem=tail_sem.at[0], recv_sem=tail_sem.at[1],
            device_id={"ch": (ch + step) % nch}, device_id_type=MESH,
        )
        for step in range(1, nch)
    ]
    for copy in to_ch:
        copy.start()
    x_pull(minus, 1, only=1), x_push(minus, 1, own2, only=1)
    x_pull(plus, 0, only=1), x_push(plus, 0, own2, only=1)
    for h in range(2):
        x_pull(two, h), x_push(two, h, own2, only=0)
    hear(4)
    for copy in local[2:]:
        copy.wait()
    project(own, True)
    project(own2)

    x_pull(minus2, 0), x_push(minus2, 0, plus, only=1)
    x_pull(plus2, 1), x_push(plus2, 1, minus, only=1)
    exchange(hsend, hrecv, h_sem)
    others = tails.at[pl.ds(0, nch - 1)]
    pltpu.make_async_copy(others, others, tail_sem.at[1]).wait()
    tail_x[...] = jnp.zeros_like(tail_x)
    for block in range(nch):
        for r in range(2):
            for part in range(tiles):
                at = pl.ds(block * feats + part * LANES, LANES)
                tail_x[pl.ds(top - 2 + r, 1), at] = tails[block, pl.ds(r * tiles + part, 1), :]
    for s in range(3):
        before = dot(tail_x[...].astype(BF16), w[s])
        proj[:top, pl.ds(s * chans, chans)] = jnp.where(ctx == 0, 0.0, before)
    x_pull(minus, 1, only=0), x_pull(plus, 0, only=0)
    for block in (two, minus, plus):
        project(block)
    for block, waits in ((minus2, (1,)), (plus2, (0,)), (two2, (0, 1))):
        for h in waits:
            x_pull(block, h)
        project(block)
    def stream(s):
        cols = pl.ds(s * chans, chans)
        return (
            taps[0, s : s + 1, :] * proj[top:, cols]
            + taps[1, s : s + 1, :] * proj[pl.ds(top - 1, rows), cols]
            + taps[2, s : s + 1, :] * proj[pl.ds(top - 2, rows), cols]
        )

    gated[...] = stream(0) * stream(2)
    gsend[...] = to_parts(gated[...]).astype(BF16)
    exchange(gsend, grecv, g_sem)
    gate[...] = stream(1)
    whole(hsend, h_sem.at[1]).wait()
    line[...] = hrecv[...].reshape(line.shape)
    forward(hspec, False)
    whole(gsend, g_sem.at[1]).wait()

    line[...] = grecv[...].astype(F32).reshape(line.shape)
    forward(spec, True)
    backward()
    csend[...] = line[...].reshape(csend.shape).astype(BF16)
    exchange(csend, crecv, c_sem)
    whole(csend, c_sem.at[1]).wait()
    y_push, y_pull, y_finish = gather(yg.at[own], yg, y_send, y_recv)
    for part, order in ((0, (own2, plus, minus)), (1, (own2, minus, plus))):
        at = pl.ds(part * LANES, LANES)
        back = crecv[:, part * OWN : (part + 1) * OWN, :].astype(F32)
        conv = back.reshape(chans, LANES).T
        mixed = gate[at, :] * (conv + skip[...] * gated[at, :])
        yg[own, at, :] = mixed.astype(BF16)
        for to in order:
            y_push(own, part, to)
    for h in range(2):
        y_push(own, h, two2, only=0)

    def mix(block):
        at = pl.ds(pl.multiple_of(block * chans, chans), chans)
        return dot(yg[block], wo[at, :])

    acc[...] = mix(own)
    y_pull(own2, 0), y_push(own2, 0, plus)
    y_pull(own2, 1), y_push(own2, 1, minus)
    y_pull(minus, 0), y_push(minus, 0, plus)
    y_pull(plus, 1), y_push(plus, 1, minus)
    y_pull(minus, 1), y_push(minus, 1, own2)
    y_pull(plus, 0), y_push(plus, 0, own2)
    for block in (own2, minus, plus):
        acc[...] += mix(block)
    y_pull(minus2, 0), y_push(minus2, 0, plus, only=1)
    y_pull(plus2, 1), y_push(plus2, 1, minus, only=1)
    for block, waits in ((two, (0, 1)), (minus2, (1,)), (plus2, (0,)), (two2, (0, 1))):
        for h in waits:
            y_pull(block, h)
        acc[...] += mix(block)
    out_ref[...] = acc[...].astype(BF16)

    x_finish()
    y_finish()
    to_next.wait_send()
    pltpu.make_async_copy(others, others, tail_sem.at[0]).wait()
    whole(hsend, h_sem.at[0]).wait()
    whole(gsend, g_sem.at[0]).wait()
    whole(csend, c_sem.at[0]).wait()


def shards(nctx, nch, inputs, in_weight, short_kernel, long_filter, skip_gain, out_weight):
    rows, feats = inputs.shape
    width, _, chans = in_weight.shape
    mixed = out_weight.shape[1]
    length = rows * nctx
    consts = [jnp.asarray(t) for t in tables(length)]
    k1 = length // LANES
    operands = [
        inputs, jnp.transpose(in_weight, (1, 0, 2)), short_kernel, long_filter,
        skip_gain.reshape(1, chans), out_weight, *consts,
    ]
    vm = pltpu.VMEM
    parts = (nctx, 2 * OWN, LANES)
    scratch = [
        vm((nch, rows, feats), BF16), vm((3, width, chans), BF16), vm(short_kernel.shape, F32),
        vm((rows, chans), F32), vm((1, chans), F32), vm(out_weight.shape, BF16),
        *[vm(c.shape, c.dtype) for c in consts],
        vm((rows + 8, 3 * chans), F32), vm((rows, chans), F32), vm((rows, chans), F32),
        vm(parts, F32), vm(parts, F32), vm(parts, BF16), vm(parts, BF16), vm(parts, BF16), vm(parts, BF16),
        vm((nch, rows, chans), BF16),
        vm((k1 * OWN, LANES), F32), vm((k1 * OWN, 2 * LANES), F32), vm((k1 * OWN, 2 * LANES), F32),
        vm((k1 * OWN, 2 * LANES), BF16), vm((k1 * OWN, 2 * LANES), BF16), vm((rows, mixed), F32),
        vm((2 * feats // LANES, LANES), F32), vm((nch, 2 * feats // LANES, LANES), F32), vm((8, width), F32),
    ]
    dma = pltpu.SemaphoreType.DMA
    sems = [
        pltpu.SemaphoreType.REGULAR((5,)), dma((10,)), dma((18,)), dma((nch, 2)), dma((2,)), dma((2,)), dma((2,)), dma((2,)), dma((2,)),
        dma((16,)), dma((nch, 2)),
    ]
    return pl.pallas_call(
        functools.partial(kernel, nctx, nch, 2),
        out_shape=pltpu.VMEM((rows, mixed), BF16),
        in_specs=[pl.BlockSpec(memory_space=pltpu.HBM)] * len(operands),
        out_specs=pl.BlockSpec(memory_space=pltpu.VMEM),
        scratch_shapes=scratch + sems,
        compiler_params=pltpu.CompilerParams(
            collective_id=0, has_side_effects=True, vmem_limit_bytes=60 * 1024 * 1024
        ),
    )(*[pltpu.with_memory_space_constraint(o, pltpu.HBM) for o in operands])


def solution(mesh):
    placed = (
        P("ctx", "ch"),
        P(None, None, "ch"),
        P(None, None, "ch"),
        P("ctx", "ch"),
        P("ch"),
        P(None, "ch"),
    )
    body = functools.partial(shards, mesh.shape["ctx"], mesh.shape["ch"])
    return jax.shard_map(body, mesh=mesh, in_specs=placed, out_specs=P("ctx", "ch"), check_vma=False)
```

```python
import functools
import math

import jax
import jax.numpy as jnp
import ml_dtypes
import numpy as np
from jax import lax
from jax.experimental import pallas as pl
from jax.experimental.pallas import tpu as pltpu
from jax.sharding import PartitionSpec as P

MESH = pl.DeviceIdType.MESH
BF16 = jnp.bfloat16
F32 = jnp.float32
LANES = 128
OWN = 8


def halves(table):
    high = table.astype(ml_dtypes.bfloat16)
    low = (table - high.astype(np.float64)).astype(ml_dtypes.bfloat16)
    return np.stack([high, low])


def tables(length):
    rows = length // LANES
    k1 = np.arange(rows)[:, None] + 0.5
    n1 = np.arange(rows)[None, :]
    n2 = np.arange(LANES)[None, :]
    k2 = np.arange(LANES)[:, None]
    outer = 2.0 * math.pi * k1 * n1 / (2 * rows)
    first = np.concatenate([np.cos(outer), -np.sin(outer)], 0)
    turn = 2.0 * math.pi * k1 * n2 / (2 * length)
    twist = np.stack([np.cos(turn), -np.sin(turn)]).astype(np.float32)
    inner = 2.0 * math.pi * k2 * n2 / LANES
    cosine, sine = np.cos(inner), np.sin(inner)
    second = np.block([[cosine, -sine], [sine, cosine]])
    back = np.block([[cosine, sine], [-sine, cosine]])
    return (
        halves(first),
        halves(first.T / length),
        np.concatenate([halves(second), halves(back)]),
        twist,
    )


def ctx_order(count):
    size = (2, count // 4, 2) if count >= 4 else (1, 1, count)
    nz = size[1]
    far = sorted(range(nz), key=lambda z: -min(z, nz - z))
    every = [(y, z, c) for z in far for y in reversed(range(size[0])) for c in reversed(range(size[2]))]
    return size, [offset for offset in every if offset != (0, 0, 0)]


def split(value):
    high = value.astype(BF16)
    return high, (value - high.astype(F32)).astype(BF16)


def dot(left, right):
    return jnp.dot(left, right, preferred_element_type=F32)


def kernel(nctx, nch, ny, *refs):
    (
        x_hbm, w_hbm, taps_hbm, filt_hbm, skip_hbm, wo_hbm,
        first_hbm, last_hbm, mid_hbm, twist_hbm,
        out_ref,
        xg, w, taps, filt, skip, wo, first, last, mid, twist,
        proj, gate, gated, hsend, hrecv, gsend, grecv, csend, crecv, yg,
        line, spec, hspec, dhi, dlo, acc, tail_out, tails, tail_x,
        heard, local_sem, x_send, x_recv, halo_sem, tail_sem, h_sem, g_sem, c_sem, y_send, y_recv,
    ) = refs
    ctx = lax.axis_index("ctx")
    ch = lax.axis_index("ch")
    rows, feats = x_hbm.shape
    chans = filt_hbm.shape[1]
    k1 = first_hbm.shape[2]

    nx = nch // ny
    half = rows // 2

    def at_ch(dx, dy):
        return ((ch // ny + dx) % nx) * ny + (ch % ny + dy) % ny

    own, plus, minus, two = at_ch(0, 0), at_ch(1, 0), at_ch(nx - 1, 0), at_ch(2, 0)
    own2, plus2, minus2, two2 = at_ch(0, 1), at_ch(1, 1), at_ch(nx - 1, 1), at_ch(2, 1)

    size, offsets = ctx_order(nctx)

    def ctx_peer(offset):
        low = ctx % size[2]
        z = (ctx // size[2]) % size[1]
        y = ctx // (size[1] * size[2])
        dy, dz, dc = offset
        return (((y + dy) % size[0]) * size[1] + (z + dz) % size[1]) * size[2] + (low + dc) % size[2]

    ctx_peers = [ctx_peer(offset) for offset in offsets]

    pairs = (
        (x_hbm, xg.at[own]), (filt_hbm, filt), (first_hbm, first), (mid_hbm, mid), (twist_hbm, twist),
        (w_hbm, w), (last_hbm, last), (taps_hbm, taps), (skip_hbm, skip), (wo_hbm, wo),
    )
    local = [pltpu.make_async_copy(s, d, local_sem.at[i]) for i, (s, d) in enumerate(pairs)]
    ways = [(0, 0, 1)] if size[2] > 1 else []
    z_ways = [(0, 1, 0), (0, size[1] - 1, 0)] if size[1] > 1 else []
    y_ways = [(1, 0, 0)] if size[0] > 1 else []
    barrier = pltpu.get_barrier_semaphore()

    def greet(sem, chs, offs):
        for to in chs:
            pl.semaphore_signal(sem, inc=1, device_id={"ch": to}, device_id_type=MESH)
        for offset in offs:
            pl.semaphore_signal(sem, inc=1, device_id={"ctx": ctx_peer(offset)}, device_id_type=MESH)

    near = (plus, minus, own2)
    rounds = [(near, ways), ((own2,), z_ways)] + [((), z_ways)] * 3

    def tell(i):
        greet(heard.at[i], *rounds[i])

    def hear(i):
        count = len(rounds[i][0]) + len(rounds[i][1])
        if count:
            pl.semaphore_wait(heard.at[i], count)

    local[0].start()
    greet(barrier, near, ways + y_ways + z_ways)
    for copy in local[1:]:
        copy.start()

    def to_parts(block):
        turned = block.T.reshape(nctx, OWN, rows)
        return jnp.concatenate([turned[:, :, :LANES], turned[:, :, LANES:]], axis=1)

    pl.semaphore_wait(barrier, len(near) + len(ways + y_ways + z_ways))


    core = ctx % size[2]

    def on(only, act):
        if only is None:
            act()
        else:
            pl.when(core == only)(act)

    def gather(source, slots, send, recv):
        started = []

        def piece(block, h):
            return slots.at[block, pl.ds(h * half, half)]

        def push(block, h, to, src=None, only=None):
            copy = pltpu.make_async_remote_copy(
                src_ref=piece(block, h) if src is None else src.at[pl.ds(h * half, half)],
                dst_ref=piece(block, h), send_sem=send.at[len(started)], recv_sem=recv.at[block, h],
                device_id={"ch": to}, device_id_type=MESH,
            )
            on(only, copy.start)
            started.append((only, copy))

        def pull(block, h, only=None):
            copy = pltpu.make_async_remote_copy(
                src_ref=piece(block, h), dst_ref=piece(block, h), send_sem=send.at[0], recv_sem=recv.at[block, h],
                device_id={"ch": own2}, device_id_type=MESH,
            )
            on(only, copy.wait_recv)

        def finish():
            for only, copy in started:
                on(only, copy.wait_send)

        return push, pull, finish

    local[0].wait()
    x_push, x_pull, x_finish = gather(x_hbm, xg, x_send, x_recv)
    for h, to in ((0, own2), (0, plus), (1, minus), (1, own2), (1, plus), (0, minus)):
        x_push(own, h, to)
    to_next = pltpu.make_async_remote_copy(
        src_ref=tail_out, dst_ref=tails.at[own], send_sem=halo_sem.at[0], recv_sem=halo_sem.at[1],
        device_id={"ctx": (ctx + 1) % nctx}, device_id_type=MESH,
    )
    tell(0)
    local[1].wait()
    hsend[...] = to_parts(filt[...])
    tiles = feats // LANES
    last_rows = xg[own, pl.ds(rows - 16, 16), :].astype(F32)
    for r in range(2):
        for part in range(tiles):
            tail_out[pl.ds(r * tiles + part, 1), :] = last_rows[14 + r : 15 + r, part * LANES : (part + 1) * LANES]
    hear(0)
    tell(1)
    hear(1)
    tell(2)
    to_next.start()


    def exchange(send, recv, sem):
        for to in ctx_peers:
            pltpu.make_async_remote_copy(
                src_ref=send.at[to], dst_ref=recv.at[ctx], send_sem=sem.at[0], recv_sem=sem.at[1],
                device_id={"ctx": to}, device_id_type=MESH,
            ).start()
        recv[pl.ds(ctx, 1)] = send[pl.ds(ctx, 1)]

    def whole(send, sem):
        part = send.at[pl.ds(0, nctx - 1)]
        return pltpu.make_async_copy(part, part, sem)

    def forward(result, exact):
        block = jnp.concatenate([line[pl.ds(c, k1, stride=OWN), :] for c in range(OWN)], axis=1)
        high, low = split(block)
        turned = dot(first[0], high) + dot(first[1], high)
        if not exact:
            turned = turned + dot(first[0], low)
        for c in range(OWN):
            real = turned[:k1, c * LANES : (c + 1) * LANES]
            imag = turned[k1:, c * LANES : (c + 1) * LANES]
            at = pl.ds(c * k1, k1)
            dhi[at, :LANES], dlo[at, :LANES] = split(real * twist[0] - imag * twist[1])
            dhi[at, LANES:], dlo[at, LANES:] = split(real * twist[1] + imag * twist[0])
        result[...] = dot(dhi[...], mid[0]) + dot(dhi[...], mid[1]) + dot(dlo[...], mid[0])

    def backward():
        xr, xi = spec[:, :LANES], spec[:, LANES:]
        hr, hi = hspec[:, :LANES], hspec[:, LANES:]
        dhi[:, :LANES], dlo[:, :LANES] = split(xr * hr - xi * hi)
        dhi[:, LANES:], dlo[:, LANES:] = split(xr * hi + xi * hr)
        spec[...] = dot(dhi[...], mid[2]) + dot(dhi[...], mid[3]) + dot(dlo[...], mid[2])
        cols = []
        for c in range(OWN):
            at = pl.ds(c * k1, k1)
            real, imag = spec[at, :LANES], spec[at, LANES:]
            cols.append(
                jnp.concatenate([real * twist[0] + imag * twist[1], imag * twist[0] - real * twist[1]], axis=0)
            )
        high, low = split(jnp.concatenate(cols, axis=1))
        signal = dot(last[0], high) + dot(last[1], high) + dot(last[0], low)
        for c in range(OWN):
            line[pl.ds(c, k1, stride=OWN), :] = signal[:, c * LANES : (c + 1) * LANES]

    top = 8

    def project(block, first_one=False):
        part = xg[block]
        at = pl.ds(pl.multiple_of(block * feats, feats), feats)
        for s in range(3):
            cols = pl.ds(s * chans, chans)
            term = dot(part, w[s, at, :])
            proj[top:, cols] = term if first_one else proj[top:, cols] + term

    x_pull(minus, 0), x_push(minus, 0, plus)
    x_pull(plus, 1), x_push(plus, 1, minus)
    hear(2)
    tell(3)
    x_pull(own2, 0), x_push(own2, 0, plus), x_push(own2, 0, minus, only=0)
    x_pull(own2, 1), x_push(own2, 1, minus), x_push(own2, 1, plus, only=0)
    hear(3)
    tell(4)
    to_next.wait_recv()
    to_ch = [
        pltpu.make_async_remote_copy(
            src_ref=tails.at[own], dst_ref=tails.at[own], send_sem=tail_sem.at[0], recv_sem=tail_sem.at[1],
            device_id={"ch": (ch + step) % nch}, device_id_type=MESH,
        )
        for step in range(1, nch)
    ]
    for copy in to_ch:
        copy.start()
    x_pull(minus, 1, only=1), x_push(minus, 1, own2, only=1)
    x_pull(plus, 0, only=1), x_push(plus, 0, own2, only=1)
    for h in range(2):
        x_pull(two, h), x_push(two, h, own2, only=0)
    hear(4)
    for copy in local[2:]:
        copy.wait()
    project(own, True)
    project(own2)

    x_pull(minus2, 0), x_push(minus2, 0, plus, only=1)
    x_pull(plus2, 1), x_push(plus2, 1, minus, only=1)
    exchange(hsend, hrecv, h_sem)
    others = tails.at[pl.ds(0, nch - 1)]
    pltpu.make_async_copy(others, others, tail_sem.at[1]).wait()
    tail_x[...] = jnp.zeros_like(tail_x)
    for block in range(nch):
        for r in range(2):
            for part in range(tiles):
                at = pl.ds(block * feats + part * LANES, LANES)
                tail_x[pl.ds(top - 2 + r, 1), at] = tails[block, pl.ds(r * tiles + part, 1), :]
    for s in range(3):
        before = dot(tail_x[...].astype(BF16), w[s])
        proj[:top, pl.ds(s * chans, chans)] = jnp.where(ctx == 0, 0.0, before)
    x_pull(minus, 1, only=0), x_pull(plus, 0, only=0)
    for block in (two, minus, plus):
        project(block)
    for block, waits in ((minus2, (1,)), (plus2, (0,)), (two2, (0, 1))):
        for h in waits:
            x_pull(block, h)
        project(block)
    def stream(s):
        cols = pl.ds(s * chans, chans)
        return (
            taps[0, s : s + 1, :] * proj[top:, cols]
            + taps[1, s : s + 1, :] * proj[pl.ds(top - 1, rows), cols]
            + taps[2, s : s + 1, :] * proj[pl.ds(top - 2, rows), cols]
        )

    gated[...] = stream(0) * stream(2)
    gsend[...] = to_parts(gated[...]).astype(BF16)
    exchange(gsend, grecv, g_sem)
    gate[...] = stream(1)
    whole(hsend, h_sem.at[1]).wait()
    line[...] = hrecv[...].reshape(line.shape)
    forward(hspec, False)
    whole(gsend, g_sem.at[1]).wait()

    line[...] = grecv[...].astype(F32).reshape(line.shape)
    forward(spec, True)
    backward()
    csend[...] = line[...].reshape(csend.shape).astype(BF16)
    exchange(csend, crecv, c_sem)
    whole(csend, c_sem.at[1]).wait()
    y_push, y_pull, y_finish = gather(yg.at[own], yg, y_send, y_recv)
    for part, order in ((0, (own2, plus, minus)), (1, (own2, minus, plus))):
        at = pl.ds(part * LANES, LANES)
        back = crecv[:, part * OWN : (part + 1) * OWN, :].astype(F32)
        conv = back.reshape(chans, LANES).T
        mixed = gate[at, :] * (conv + skip[...] * gated[at, :])
        yg[own, at, :] = mixed.astype(BF16)
        for to in order:
            y_push(own, part, to)
    for h in range(2):
        y_push(own, h, two2, only=0)

    def mix(block):
        at = pl.ds(pl.multiple_of(block * chans, chans), chans)
        return dot(yg[block], wo[at, :])

    acc[...] = mix(own)
    y_pull(own2, 0), y_push(own2, 0, plus)
    y_pull(own2, 1), y_push(own2, 1, minus)
    y_pull(minus, 0), y_push(minus, 0, plus)
    y_pull(plus, 1), y_push(plus, 1, minus)
    y_pull(minus, 1), y_push(minus, 1, own2)
    y_pull(plus, 0), y_push(plus, 0, own2)
    for block in (own2, minus, plus):
        acc[...] += mix(block)
    y_pull(minus2, 0), y_push(minus2, 0, plus, only=1)
    y_pull(plus2, 1), y_push(plus2, 1, minus, only=1)
    for block, waits in ((two, (0, 1)), (minus2, (1,)), (plus2, (0,)), (two2, (0, 1))):
        for h in waits:
            y_pull(block, h)
        acc[...] += mix(block)
    out_ref[...] = acc[...].astype(BF16)

    x_finish()
    y_finish()
    to_next.wait_send()
    pltpu.make_async_copy(others, others, tail_sem.at[0]).wait()
    whole(hsend, h_sem.at[0]).wait()
    whole(gsend, g_sem.at[0]).wait()
    whole(csend, c_sem.at[0]).wait()


def shards(nctx, nch, inputs, in_weight, short_kernel, long_filter, skip_gain, out_weight):
    rows, feats = inputs.shape
    width, _, chans = in_weight.shape
    mixed = out_weight.shape[1]
    length = rows * nctx
    consts = [jnp.asarray(t) for t in tables(length)]
    k1 = length // LANES
    operands = [
        inputs, jnp.transpose(in_weight, (1, 0, 2)), short_kernel, long_filter,
        skip_gain.reshape(1, chans), out_weight, *consts,
    ]
    vm = pltpu.VMEM
    parts = (nctx, 2 * OWN, LANES)
    scratch = [
        vm((nch, rows, feats), BF16), vm((3, width, chans), BF16), vm(short_kernel.shape, F32),
        vm((rows, chans), F32), vm((1, chans), F32), vm(out_weight.shape, BF16),
        *[vm(c.shape, c.dtype) for c in consts],
        vm((rows + 8, 3 * chans), F32), vm((rows, chans), F32), vm((rows, chans), F32),
        vm(parts, F32), vm(parts, F32), vm(parts, BF16), vm(parts, BF16), vm(parts, BF16), vm(parts, BF16),
        vm((nch, rows, chans), BF16),
        vm((k1 * OWN, LANES), F32), vm((k1 * OWN, 2 * LANES), F32), vm((k1 * OWN, 2 * LANES), F32),
        vm((k1 * OWN, 2 * LANES), BF16), vm((k1 * OWN, 2 * LANES), BF16), vm((rows, mixed), F32),
        vm((2 * feats // LANES, LANES), F32), vm((nch, 2 * feats // LANES, LANES), F32), vm((8, width), F32),
    ]
    dma = pltpu.SemaphoreType.DMA
    sems = [
        pltpu.SemaphoreType.REGULAR((5,)), dma((10,)), dma((18,)), dma((nch, 2)), dma((2,)), dma((2,)), dma((2,)), dma((2,)), dma((2,)),
        dma((16,)), dma((nch, 2)),
    ]
    return pl.pallas_call(
        functools.partial(kernel, nctx, nch, 2),
        out_shape=pltpu.VMEM((rows, mixed), BF16),
        in_specs=[pl.BlockSpec(memory_space=pltpu.HBM)] * len(operands),
        out_specs=pl.BlockSpec(memory_space=pltpu.VMEM),
        scratch_shapes=scratch + sems,
        compiler_params=pltpu.CompilerParams(
            collective_id=0, has_side_effects=True, vmem_limit_bytes=60 * 1024 * 1024
        ),
    )(*[pltpu.with_memory_space_constraint(o, pltpu.HBM) for o in operands])


def solution(mesh):
    placed = (
        P("ctx", "ch"),
        P(None, None, "ch"),
        P(None, None, "ch"),
        P("ctx", "ch"),
        P("ch"),
        P(None, "ch"),
    )
    body = functools.partial(shards, mesh.shape["ctx"], mesh.shape["ch"])
    return jax.shard_map(body, mesh=mesh, in_specs=placed, out_specs=P("ctx", "ch"), check_vma=False)
```

```python
import functools
import math

import jax
import jax.numpy as jnp
import ml_dtypes
import numpy as np
from jax import lax
from jax.experimental import pallas as pl
from jax.experimental.pallas import tpu as pltpu
from jax.sharding import PartitionSpec as P

MESH = pl.DeviceIdType.MESH
BF16 = jnp.bfloat16
F32 = jnp.float32
LANES = 128
OWN = 8


def halves(table):
    high = table.astype(ml_dtypes.bfloat16)
    low = (table - high.astype(np.float64)).astype(ml_dtypes.bfloat16)
    return np.stack([high, low])


def tables(length):
    rows = length // LANES
    k1 = np.arange(rows)[:, None] + 0.5
    n1 = np.arange(rows)[None, :]
    n2 = np.arange(LANES)[None, :]
    k2 = np.arange(LANES)[:, None]
    outer = 2.0 * math.pi * k1 * n1 / (2 * rows)
    first = np.concatenate([np.cos(outer), -np.sin(outer)], 0)
    turn = 2.0 * math.pi * k1 * n2 / (2 * length)
    twist = np.stack([np.cos(turn), -np.sin(turn)]).astype(np.float32)
    inner = 2.0 * math.pi * k2 * n2 / LANES
    cosine, sine = np.cos(inner), np.sin(inner)
    second = np.block([[cosine, -sine], [sine, cosine]])
    back = np.block([[cosine, sine], [-sine, cosine]])
    return (
        halves(first),
        halves(first.T / length),
        np.concatenate([halves(second), halves(back)]),
        twist,
    )


def ctx_order(count):
    size = (2, count // 4, 2) if count >= 4 else (1, 1, count)
    nz = size[1]
    far = sorted(range(nz), key=lambda z: -min(z, nz - z))
    every = [(y, z, c) for z in far for y in reversed(range(size[0])) for c in reversed(range(size[2]))]
    return size, [offset for offset in every if offset != (0, 0, 0)]


def split(value):
    high = value.astype(BF16)
    return high, (value - high.astype(F32)).astype(BF16)


def dot(left, right):
    return jnp.dot(left, right, preferred_element_type=F32)


def kernel(nctx, nch, ny, *refs):
    (
        x_hbm, w_hbm, taps_hbm, filt_hbm, skip_hbm, wo_hbm,
        first_hbm, last_hbm, mid_hbm, twist_hbm,
        out_ref,
        xg, w, taps, filt, skip, wo, first, last, mid, twist,
        proj, gate, gated, hsend, hrecv, gsend, grecv, csend, crecv, yg,
        line, spec, hspec, dhi, dlo, acc, tail_out, tails, tail_x,
        heard, local_sem, x_send, x_recv, halo_sem, tail_sem, h_sem, g_sem, c_sem, y_send, y_recv,
    ) = refs
    ctx = lax.axis_index("ctx")
    ch = lax.axis_index("ch")
    rows, feats = x_hbm.shape
    chans = filt_hbm.shape[1]
    k1 = first_hbm.shape[2]

    nx = nch // ny
    half = rows // 2

    def at_ch(dx, dy):
        return ((ch // ny + dx) % nx) * ny + (ch % ny + dy) % ny

    own, plus, minus, two = at_ch(0, 0), at_ch(1, 0), at_ch(nx - 1, 0), at_ch(2, 0)
    own2, plus2, minus2, two2 = at_ch(0, 1), at_ch(1, 1), at_ch(nx - 1, 1), at_ch(2, 1)

    size, offsets = ctx_order(nctx)

    def ctx_peer(offset):
        low = ctx % size[2]
        z = (ctx // size[2]) % size[1]
        y = ctx // (size[1] * size[2])
        dy, dz, dc = offset
        return (((y + dy) % size[0]) * size[1] + (z + dz) % size[1]) * size[2] + (low + dc) % size[2]

    ctx_peers = [ctx_peer(offset) for offset in offsets]

    pairs = (
        (x_hbm, xg.at[own]), (filt_hbm, filt), (first_hbm, first), (mid_hbm, mid), (twist_hbm, twist),
        (w_hbm, w), (last_hbm, last), (taps_hbm, taps), (skip_hbm, skip), (wo_hbm, wo),
    )
    local = [pltpu.make_async_copy(s, d, local_sem.at[i]) for i, (s, d) in enumerate(pairs)]
    ways = [(0, 0, 1)] if size[2] > 1 else []
    z_ways = [(0, 1, 0), (0, size[1] - 1, 0)] if size[1] > 1 else []
    y_ways = [(1, 0, 0)] if size[0] > 1 else []
    barrier = pltpu.get_barrier_semaphore()

    def greet(sem, chs, offs):
        for to in chs:
            pl.semaphore_signal(sem, inc=1, device_id={"ch": to}, device_id_type=MESH)
        for offset in offs:
            pl.semaphore_signal(sem, inc=1, device_id={"ctx": ctx_peer(offset)}, device_id_type=MESH)

    near = (plus, minus, own2)
    rounds = [(near, ways), ((own2,), z_ways)] + [((), z_ways)] * 3

    def tell(i):
        greet(heard.at[i], *rounds[i])

    def hear(i):
        count = len(rounds[i][0]) + len(rounds[i][1])
        if count:
            pl.semaphore_wait(heard.at[i], count)

    local[0].start()
    greet(barrier, near, ways + y_ways + z_ways)
    for copy in local[1:]:
        copy.start()

    def to_parts(block):
        turned = block.T.reshape(nctx, OWN, rows)
        return jnp.concatenate([turned[:, :, :LANES], turned[:, :, LANES:]], axis=1)

    pl.semaphore_wait(barrier, len(near) + len(ways + y_ways + z_ways))


    core = ctx % size[2]

    def on(only, act):
        if only is None:
            act()
        else:
            pl.when(core == only)(act)

    def gather(source, slots, send, recv):
        started = []

        def piece(block, h):
            return slots.at[block, pl.ds(h * half, half)]

        def push(block, h, to, src=None, only=None):
            copy = pltpu.make_async_remote_copy(
                src_ref=piece(block, h) if src is None else src.at[pl.ds(h * half, half)],
                dst_ref=piece(block, h), send_sem=send.at[len(started)], recv_sem=recv.at[block, h],
                device_id={"ch": to}, device_id_type=MESH,
            )
            on(only, copy.start)
            started.append((only, copy))

        def pull(block, h, only=None):
            copy = pltpu.make_async_remote_copy(
                src_ref=piece(block, h), dst_ref=piece(block, h), send_sem=send.at[0], recv_sem=recv.at[block, h],
                device_id={"ch": own2}, device_id_type=MESH,
            )
            on(only, copy.wait_recv)

        def finish():
            for only, copy in started:
                on(only, copy.wait_send)

        return push, pull, finish

    local[0].wait()
    x_push, x_pull, x_finish = gather(x_hbm, xg, x_send, x_recv)
    for h, to in ((0, own2), (0, plus), (1, minus), (1, own2), (1, plus), (0, minus)):
        x_push(own, h, to)
    to_next = pltpu.make_async_remote_copy(
        src_ref=tail_out, dst_ref=tails.at[own], send_sem=halo_sem.at[0], recv_sem=halo_sem.at[1],
        device_id={"ctx": (ctx + 1) % nctx}, device_id_type=MESH,
    )
    tell(0)
    local[1].wait()
    hsend[...] = to_parts(filt[...])
    tiles = feats // LANES
    last_rows = xg[own, pl.ds(rows - 16, 16), :].astype(F32)
    for r in range(2):
        for part in range(tiles):
            tail_out[pl.ds(r * tiles + part, 1), :] = last_rows[14 + r : 15 + r, part * LANES : (part + 1) * LANES]
    hear(0)
    tell(1)
    hear(1)
    tell(2)
    to_next.start()


    def exchange(send, recv, sem):
        for to in ctx_peers:
            pltpu.make_async_remote_copy(
                src_ref=send.at[to], dst_ref=recv.at[ctx], send_sem=sem.at[0], recv_sem=sem.at[1],
                device_id={"ctx": to}, device_id_type=MESH,
            ).start()
        recv[pl.ds(ctx, 1)] = send[pl.ds(ctx, 1)]

    def whole(send, sem):
        part = send.at[pl.ds(0, nctx - 1)]
        return pltpu.make_async_copy(part, part, sem)

    def forward(result, exact):
        block = jnp.concatenate([line[pl.ds(c, k1, stride=OWN), :] for c in range(OWN)], axis=1)
        high, low = split(block)
        turned = dot(first[0], high) + dot(first[1], high)
        if not exact:
            turned = turned + dot(first[0], low)
        for c in range(OWN):
            real = turned[:k1, c * LANES : (c + 1) * LANES]
            imag = turned[k1:, c * LANES : (c + 1) * LANES]
            at = pl.ds(c * k1, k1)
            dhi[at, :LANES], dlo[at, :LANES] = split(real * twist[0] - imag * twist[1])
            dhi[at, LANES:], dlo[at, LANES:] = split(real * twist[1] + imag * twist[0])
        result[...] = dot(dhi[...], mid[0]) + dot(dhi[...], mid[1]) + dot(dlo[...], mid[0])

    def backward():
        xr, xi = spec[:, :LANES], spec[:, LANES:]
        hr, hi = hspec[:, :LANES], hspec[:, LANES:]
        dhi[:, :LANES], dlo[:, :LANES] = split(xr * hr - xi * hi)
        dhi[:, LANES:], dlo[:, LANES:] = split(xr * hi + xi * hr)
        spec[...] = dot(dhi[...], mid[2]) + dot(dhi[...], mid[3]) + dot(dlo[...], mid[2])
        cols = []
        for c in range(OWN):
            at = pl.ds(c * k1, k1)
            real, imag = spec[at, :LANES], spec[at, LANES:]
            cols.append(
                jnp.concatenate([real * twist[0] + imag * twist[1], imag * twist[0] - real * twist[1]], axis=0)
            )
        high, low = split(jnp.concatenate(cols, axis=1))
        signal = dot(last[0], high) + dot(last[1], high) + dot(last[0], low)
        for c in range(OWN):
            line[pl.ds(c, k1, stride=OWN), :] = signal[:, c * LANES : (c + 1) * LANES]

    top = 8

    def project(block, first_one=False):
        part = xg[block]
        at = pl.ds(pl.multiple_of(block * feats, feats), feats)
        for s in range(3):
            cols = pl.ds(s * chans, chans)
            term = dot(part, w[s, at, :])
            proj[top:, cols] = term if first_one else proj[top:, cols] + term

    x_pull(minus, 0), x_push(minus, 0, plus)
    x_pull(plus, 1), x_push(plus, 1, minus)
    hear(2)
    tell(3)
    x_pull(own2, 0), x_push(own2, 0, plus), x_push(own2, 0, minus, only=0)
    x_pull(own2, 1), x_push(own2, 1, minus), x_push(own2, 1, plus, only=0)
    hear(3)
    tell(4)
    to_next.wait_recv()
    to_ch = [
        pltpu.make_async_remote_copy(
            src_ref=tails.at[own], dst_ref=tails.at[own], send_sem=tail_sem.at[0], recv_sem=tail_sem.at[1],
            device_id={"ch": (ch + step) % nch}, device_id_type=MESH,
        )
        for step in range(1, nch)
    ]
    for copy in to_ch:
        copy.start()
    x_pull(minus, 1, only=1), x_push(minus, 1, own2, only=1)
    x_pull(plus, 0, only=1), x_push(plus, 0, own2, only=1)
    for h in range(2):
        x_pull(two, h), x_push(two, h, own2, only=0)
    hear(4)
    for copy in local[2:]:
        copy.wait()
    project(own, True)
    project(own2)

    x_pull(minus2, 0), x_push(minus2, 0, plus, only=1)
    x_pull(plus2, 1), x_push(plus2, 1, minus, only=1)
    exchange(hsend, hrecv, h_sem)
    others = tails.at[pl.ds(0, nch - 1)]
    pltpu.make_async_copy(others, others, tail_sem.at[1]).wait()
    tail_x[...] = jnp.zeros_like(tail_x)
    for block in range(nch):
        for r in range(2):
            for part in range(tiles):
                at = pl.ds(block * feats + part * LANES, LANES)
                tail_x[pl.ds(top - 2 + r, 1), at] = tails[block, pl.ds(r * tiles + part, 1), :]
    for s in range(3):
        before = dot(tail_x[...].astype(BF16), w[s])
        proj[:top, pl.ds(s * chans, chans)] = jnp.where(ctx == 0, 0.0, before)
    x_pull(minus, 1, only=0), x_pull(plus, 0, only=0)
    for block in (two, minus, plus):
        project(block)
    for block, waits in ((minus2, (1,)), (plus2, (0,)), (two2, (0, 1))):
        for h in waits:
            x_pull(block, h)
        project(block)
    def stream(s):
        cols = pl.ds(s * chans, chans)
        return (
            taps[0, s : s + 1, :] * proj[top:, cols]
            + taps[1, s : s + 1, :] * proj[pl.ds(top - 1, rows), cols]
            + taps[2, s : s + 1, :] * proj[pl.ds(top - 2, rows), cols]
        )

    gated[...] = stream(0) * stream(2)
    gsend[...] = to_parts(gated[...]).astype(BF16)
    exchange(gsend, grecv, g_sem)
    gate[...] = stream(1)
    whole(hsend, h_sem.at[1]).wait()
    line[...] = hrecv[...].reshape(line.shape)
    forward(hspec, False)
    whole(gsend, g_sem.at[1]).wait()

    line[...] = grecv[...].astype(F32).reshape(line.shape)
    forward(spec, True)
    backward()
    csend[...] = line[...].reshape(csend.shape).astype(BF16)
    exchange(csend, crecv, c_sem)
    whole(csend, c_sem.at[1]).wait()
    y_push, y_pull, y_finish = gather(yg.at[own], yg, y_send, y_recv)
    back = crecv[...].astype(F32)
    for part, order in ((0, (own2, plus, minus)), (1, (own2, minus, plus))):
        at = pl.ds(part * LANES, LANES)
        conv = back[:, part * OWN : (part + 1) * OWN, :].reshape(chans, LANES).T
        mixed = gate[at, :] * (conv + skip[...] * gated[at, :])
        yg[own, at, :] = mixed.astype(BF16)
        for to in order:
            y_push(own, part, to)
    for h in range(2):
        y_push(own, h, two2, only=0)

    def mix(block):
        at = pl.ds(pl.multiple_of(block * chans, chans), chans)
        return dot(yg[block], wo[at, :])

    acc[...] = mix(own)
    y_pull(own2, 0), y_push(own2, 0, plus)
    y_pull(own2, 1), y_push(own2, 1, minus)
    y_pull(minus, 0), y_push(minus, 0, plus)
    y_pull(plus, 1), y_push(plus, 1, minus)
    y_pull(minus, 1), y_push(minus, 1, own2)
    y_pull(plus, 0), y_push(plus, 0, own2)
    for block in (own2, minus, plus):
        acc[...] += mix(block)
    y_pull(minus2, 0), y_push(minus2, 0, plus, only=1)
    y_pull(plus2, 1), y_push(plus2, 1, minus, only=1)
    for block, waits in ((two, (0, 1)), (minus2, (1,)), (plus2, (0,)), (two2, (0, 1))):
        for h in waits:
            y_pull(block, h)
        acc[...] += mix(block)
    out_ref[...] = acc[...].astype(BF16)

    x_finish()
    y_finish()
    to_next.wait_send()
    pltpu.make_async_copy(others, others, tail_sem.at[0]).wait()
    whole(hsend, h_sem.at[0]).wait()
    whole(gsend, g_sem.at[0]).wait()
    whole(csend, c_sem.at[0]).wait()


def shards(nctx, nch, inputs, in_weight, short_kernel, long_filter, skip_gain, out_weight):
    rows, feats = inputs.shape
    width, _, chans = in_weight.shape
    mixed = out_weight.shape[1]
    length = rows * nctx
    consts = [jnp.asarray(t) for t in tables(length)]
    k1 = length // LANES
    operands = [
        inputs, jnp.transpose(in_weight, (1, 0, 2)), short_kernel, long_filter,
        skip_gain.reshape(1, chans), out_weight, *consts,
    ]
    vm = pltpu.VMEM
    parts = (nctx, 2 * OWN, LANES)
    scratch = [
        vm((nch, rows, feats), BF16), vm((3, width, chans), BF16), vm(short_kernel.shape, F32),
        vm((rows, chans), F32), vm((1, chans), F32), vm(out_weight.shape, BF16),
        *[vm(c.shape, c.dtype) for c in consts],
        vm((rows + 8, 3 * chans), F32), vm((rows, chans), F32), vm((rows, chans), F32),
        vm(parts, F32), vm(parts, F32), vm(parts, BF16), vm(parts, BF16), vm(parts, BF16), vm(parts, BF16),
        vm((nch, rows, chans), BF16),
        vm((k1 * OWN, LANES), F32), vm((k1 * OWN, 2 * LANES), F32), vm((k1 * OWN, 2 * LANES), F32),
        vm((k1 * OWN, 2 * LANES), BF16), vm((k1 * OWN, 2 * LANES), BF16), vm((rows, mixed), F32),
        vm((2 * feats // LANES, LANES), F32), vm((nch, 2 * feats // LANES, LANES), F32), vm((8, width), F32),
    ]
    dma = pltpu.SemaphoreType.DMA
    sems = [
        pltpu.SemaphoreType.REGULAR((5,)), dma((10,)), dma((18,)), dma((nch, 2)), dma((2,)), dma((2,)), dma((2,)), dma((2,)), dma((2,)),
        dma((16,)), dma((nch, 2)),
    ]
    return pl.pallas_call(
        functools.partial(kernel, nctx, nch, 2),
        out_shape=pltpu.VMEM((rows, mixed), BF16),
        in_specs=[pl.BlockSpec(memory_space=pltpu.HBM)] * len(operands),
        out_specs=pl.BlockSpec(memory_space=pltpu.VMEM),
        scratch_shapes=scratch + sems,
        compiler_params=pltpu.CompilerParams(
            collective_id=0, has_side_effects=True, vmem_limit_bytes=60 * 1024 * 1024
        ),
    )(*[pltpu.with_memory_space_constraint(o, pltpu.HBM) for o in operands])


def solution(mesh):
    placed = (
        P("ctx", "ch"),
        P(None, None, "ch"),
        P(None, None, "ch"),
        P("ctx", "ch"),
        P("ch"),
        P(None, "ch"),
    )
    body = functools.partial(shards, mesh.shape["ctx"], mesh.shape["ch"])
    return jax.shard_map(body, mesh=mesh, in_specs=placed, out_specs=P("ctx", "ch"), check_vma=False)
```

```python
import functools
import math

import jax
import jax.numpy as jnp
import ml_dtypes
import numpy as np
from jax import lax
from jax.experimental import pallas as pl
from jax.experimental.pallas import tpu as pltpu
from jax.sharding import PartitionSpec as P

MESH = pl.DeviceIdType.MESH
BF16 = jnp.bfloat16
F32 = jnp.float32
LANES = 128
OWN = 8


def halves(table):
    high = table.astype(ml_dtypes.bfloat16)
    low = (table - high.astype(np.float64)).astype(ml_dtypes.bfloat16)
    return np.stack([high, low])


def tables(length):
    rows = length // LANES
    k1 = np.arange(rows)[:, None] + 0.5
    n1 = np.arange(rows)[None, :]
    n2 = np.arange(LANES)[None, :]
    k2 = np.arange(LANES)[:, None]
    outer = 2.0 * math.pi * k1 * n1 / (2 * rows)
    first = np.concatenate([np.cos(outer), -np.sin(outer)], 0)
    turn = 2.0 * math.pi * k1 * n2 / (2 * length)
    twist = np.stack([np.cos(turn), -np.sin(turn)]).astype(np.float32)
    inner = 2.0 * math.pi * k2 * n2 / LANES
    cosine, sine = np.cos(inner), np.sin(inner)
    second = np.block([[cosine, -sine], [sine, cosine]])
    back = np.block([[cosine, sine], [-sine, cosine]])
    return (
        np.concatenate(list(halves(first)), 1),
        np.concatenate([halves(first.T / length)[i] for i in (0, 1, 0)], 1),
        np.stack([np.concatenate([halves(t)[i] for i in (0, 0, 1)]) for t in (second, back)]),
        twist,
    )


def ctx_order(count):
    size = (2, count // 4, 2) if count >= 4 else (1, 1, count)
    nz = size[1]
    far = sorted(range(nz), key=lambda z: -min(z, nz - z))
    every = [(y, z, c) for z in far for y in reversed(range(size[0])) for c in reversed(range(size[2]))]
    return size, [offset for offset in every if offset != (0, 0, 0)]


def split(value):
    high = value.astype(BF16)
    return high, (value - high.astype(F32)).astype(BF16)


def dot(left, right):
    return jnp.dot(left, right, preferred_element_type=F32)


def kernel(nctx, nch, ny, *refs):
    (
        x_hbm, w_hbm, taps_hbm, filt_hbm, skip_hbm, wo_hbm,
        first_hbm, last_hbm, mid_hbm, twist_hbm,
        out_ref,
        xg, w, taps, filt, skip, wo, first, last, mid, twist,
        proj, gate, gated, hsend, hrecv, gsend, grecv, csend, crecv, yg,
        line, spec, hspec, parts3, acc, tail_out, tails, tail_x,
        heard, local_sem, x_send, x_recv, halo_sem, tail_sem, h_sem, g_sem, c_sem, y_send, y_recv,
    ) = refs
    ctx = lax.axis_index("ctx")
    ch = lax.axis_index("ch")
    rows, feats = x_hbm.shape
    chans = filt_hbm.shape[1]
    k1 = first_hbm.shape[0] // 2

    nx = nch // ny
    half = rows // 2

    def at_ch(dx, dy):
        return ((ch // ny + dx) % nx) * ny + (ch % ny + dy) % ny

    own, plus, minus, two = at_ch(0, 0), at_ch(1, 0), at_ch(nx - 1, 0), at_ch(2, 0)
    own2, plus2, minus2, two2 = at_ch(0, 1), at_ch(1, 1), at_ch(nx - 1, 1), at_ch(2, 1)

    size, offsets = ctx_order(nctx)

    def ctx_peer(offset):
        low = ctx % size[2]
        z = (ctx // size[2]) % size[1]
        y = ctx // (size[1] * size[2])
        dy, dz, dc = offset
        return (((y + dy) % size[0]) * size[1] + (z + dz) % size[1]) * size[2] + (low + dc) % size[2]

    ctx_peers = [ctx_peer(offset) for offset in offsets]

    pairs = (
        (x_hbm, xg.at[own]), (filt_hbm, filt), (first_hbm, first), (mid_hbm, mid), (twist_hbm, twist),
        (w_hbm, w), (last_hbm, last), (taps_hbm, taps), (skip_hbm, skip), (wo_hbm, wo),
    )
    local = [pltpu.make_async_copy(s, d, local_sem.at[i]) for i, (s, d) in enumerate(pairs)]
    ways = [(0, 0, 1)] if size[2] > 1 else []
    z_ways = [(0, 1, 0), (0, size[1] - 1, 0)] if size[1] > 1 else []
    y_ways = [(1, 0, 0)] if size[0] > 1 else []
    barrier = pltpu.get_barrier_semaphore()

    def greet(sem, chs, offs):
        for to in chs:
            pl.semaphore_signal(sem, inc=1, device_id={"ch": to}, device_id_type=MESH)
        for offset in offs:
            pl.semaphore_signal(sem, inc=1, device_id={"ctx": ctx_peer(offset)}, device_id_type=MESH)

    near = (plus, minus, own2)
    rounds = [(near, ways), ((own2,), z_ways)] + [((), z_ways)] * 3

    def tell(i):
        greet(heard.at[i], *rounds[i])

    def hear(i):
        count = len(rounds[i][0]) + len(rounds[i][1])
        if count:
            pl.semaphore_wait(heard.at[i], count)

    local[0].start()
    greet(barrier, near, ways + y_ways + z_ways)
    for copy in local[1:]:
        copy.start()

    def to_parts(block):
        turned = block.T.reshape(nctx, OWN, rows)
        return jnp.concatenate([turned[:, :, :LANES], turned[:, :, LANES:]], axis=1)

    pl.semaphore_wait(barrier, len(near) + len(ways + y_ways + z_ways))


    core = ctx % size[2]

    def on(only, act):
        if only is None:
            act()
        else:
            pl.when(core == only)(act)

    def gather(source, slots, send, recv):
        started = []

        def piece(block, h):
            return slots.at[block, pl.ds(h * half, half)]

        def push(block, h, to, src=None, only=None):
            copy = pltpu.make_async_remote_copy(
                src_ref=piece(block, h) if src is None else src.at[pl.ds(h * half, half)],
                dst_ref=piece(block, h), send_sem=send.at[len(started)], recv_sem=recv.at[block, h],
                device_id={"ch": to}, device_id_type=MESH,
            )
            on(only, copy.start)
            started.append((only, copy))

        def pull(block, h, only=None):
            copy = pltpu.make_async_remote_copy(
                src_ref=piece(block, h), dst_ref=piece(block, h), send_sem=send.at[0], recv_sem=recv.at[block, h],
                device_id={"ch": own2}, device_id_type=MESH,
            )
            on(only, copy.wait_recv)

        def finish():
            for only, copy in started:
                on(only, copy.wait_send)

        return push, pull, finish

    local[0].wait()
    x_push, x_pull, x_finish = gather(x_hbm, xg, x_send, x_recv)
    for h, to in ((0, own2), (0, plus), (1, minus), (1, own2), (1, plus), (0, minus)):
        x_push(own, h, to)
    to_next = pltpu.make_async_remote_copy(
        src_ref=tail_out, dst_ref=tails.at[own], send_sem=halo_sem.at[0], recv_sem=halo_sem.at[1],
        device_id={"ctx": (ctx + 1) % nctx}, device_id_type=MESH,
    )
    tell(0)
    local[1].wait()
    hsend[...] = to_parts(filt[...])
    tiles = feats // LANES
    last_rows = xg[own, pl.ds(rows - 16, 16), :].astype(F32)
    for r in range(2):
        for part in range(tiles):
            tail_out[pl.ds(r * tiles + part, 1), :] = last_rows[14 + r : 15 + r, part * LANES : (part + 1) * LANES]
    hear(0)
    tell(1)
    hear(1)
    tell(2)
    to_next.start()


    def exchange(send, recv, sem):
        for to in ctx_peers:
            pltpu.make_async_remote_copy(
                src_ref=send.at[to], dst_ref=recv.at[ctx], send_sem=sem.at[0], recv_sem=sem.at[1],
                device_id={"ctx": to}, device_id_type=MESH,
            ).start()
        recv[pl.ds(ctx, 1)] = send[pl.ds(ctx, 1)]

    def whole(send, sem):
        part = send.at[pl.ds(0, nctx - 1)]
        return pltpu.make_async_copy(part, part, sem)

    def lay(at, col, value):
        high, low = split(value)
        for i, half_value in enumerate((high, low, high)):
            parts3[at, col + 2 * LANES * i : col + 2 * LANES * i + LANES] = half_value

    def forward(result, exact):
        block = jnp.concatenate([line[pl.ds(c, k1, stride=OWN), :] for c in range(OWN)], axis=1)
        high, low = split(block)
        turned = dot(first[...], jnp.concatenate([high, high], axis=0))
        if not exact:
            turned = turned + dot(first[...], jnp.concatenate([low, jnp.zeros_like(low)], axis=0))
        for c in range(OWN):
            real = turned[:k1, c * LANES : (c + 1) * LANES]
            imag = turned[k1:, c * LANES : (c + 1) * LANES]
            at = pl.ds(c * k1, k1)
            lay(at, 0, real * twist[0] - imag * twist[1])
            lay(at, LANES, real * twist[1] + imag * twist[0])
        result[...] = dot(parts3[...], mid[0])

    def backward():
        xr, xi = spec[:, :LANES], spec[:, LANES:]
        hr, hi = hspec[:, :LANES], hspec[:, LANES:]
        every = slice(None)
        lay(every, 0, xr * hr - xi * hi)
        lay(every, LANES, xr * hi + xi * hr)
        spec[...] = dot(parts3[...], mid[1])
        cols = []
        for c in range(OWN):
            at = pl.ds(c * k1, k1)
            real, imag = spec[at, :LANES], spec[at, LANES:]
            cols.append(
                jnp.concatenate([real * twist[0] + imag * twist[1], imag * twist[0] - real * twist[1]], axis=0)
            )
        high, low = split(jnp.concatenate(cols, axis=1))
        signal = dot(last[...], jnp.concatenate([high, high, low], axis=0))
        for c in range(OWN):
            line[pl.ds(c, k1, stride=OWN), :] = signal[:, c * LANES : (c + 1) * LANES]

    top = 8

    def project(block, first_one=False):
        part = xg[block]
        at = pl.ds(pl.multiple_of(block * feats, feats), feats)
        for s in range(3):
            cols = pl.ds(s * chans, chans)
            term = dot(part, w[s, at, :])
            proj[top:, cols] = term if first_one else proj[top:, cols] + term

    x_pull(minus, 0), x_push(minus, 0, plus)
    x_pull(plus, 1), x_push(plus, 1, minus)
    hear(2)
    tell(3)
    x_pull(own2, 0), x_push(own2, 0, plus), x_push(own2, 0, minus, only=0)
    x_pull(own2, 1), x_push(own2, 1, minus), x_push(own2, 1, plus, only=0)
    hear(3)
    tell(4)
    to_next.wait_recv()
    to_ch = [
        pltpu.make_async_remote_copy(
            src_ref=tails.at[own], dst_ref=tails.at[own], send_sem=tail_sem.at[0], recv_sem=tail_sem.at[1],
            device_id={"ch": (ch + step) % nch}, device_id_type=MESH,
        )
        for step in range(1, nch)
    ]
    for copy in to_ch:
        copy.start()
    x_pull(minus, 1, only=1), x_push(minus, 1, own2, only=1)
    x_pull(plus, 0, only=1), x_push(plus, 0, own2, only=1)
    for h in range(2):
        x_pull(two, h), x_push(two, h, own2, only=0)
    hear(4)
    for copy in local[2:]:
        copy.wait()
    project(own, True)
    project(own2)

    x_pull(minus2, 0), x_push(minus2, 0, plus, only=1)
    x_pull(plus2, 1), x_push(plus2, 1, minus, only=1)
    exchange(hsend, hrecv, h_sem)
    others = tails.at[pl.ds(0, nch - 1)]
    pltpu.make_async_copy(others, others, tail_sem.at[1]).wait()
    tail_x[...] = jnp.zeros_like(tail_x)
    for block in range(nch):
        for r in range(2):
            for part in range(tiles):
                at = pl.ds(block * feats + part * LANES, LANES)
                tail_x[pl.ds(top - 2 + r, 1), at] = tails[block, pl.ds(r * tiles + part, 1), :]
    for s in range(3):
        before = dot(tail_x[...].astype(BF16), w[s])
        proj[:top, pl.ds(s * chans, chans)] = jnp.where(ctx == 0, 0.0, before)
    x_pull(minus, 1, only=0), x_pull(plus, 0, only=0)
    for block in (two, minus, plus):
        project(block)
    for block, waits in ((minus2, (1,)), (plus2, (0,)), (two2, (0, 1))):
        for h in waits:
            x_pull(block, h)
        project(block)
    def stream(s):
        cols = pl.ds(s * chans, chans)
        return (
            taps[0, s : s + 1, :] * proj[top:, cols]
            + taps[1, s : s + 1, :] * proj[pl.ds(top - 1, rows), cols]
            + taps[2, s : s + 1, :] * proj[pl.ds(top - 2, rows), cols]
        )

    gated[...] = stream(0) * stream(2)
    gsend[...] = to_parts(gated[...]).astype(BF16)
    exchange(gsend, grecv, g_sem)
    gate[...] = stream(1)
    whole(hsend, h_sem.at[1]).wait()
    line[...] = hrecv[...].reshape(line.shape)
    forward(hspec, False)
    whole(gsend, g_sem.at[1]).wait()

    line[...] = grecv[...].astype(F32).reshape(line.shape)
    forward(spec, True)
    backward()
    csend[...] = line[...].reshape(csend.shape).astype(BF16)
    exchange(csend, crecv, c_sem)
    whole(csend, c_sem.at[1]).wait()
    y_push, y_pull, y_finish = gather(yg.at[own], yg, y_send, y_recv)
    back = crecv[...].astype(F32)
    for part, order in ((0, (own2, plus, minus)), (1, (own2, minus, plus))):
        at = pl.ds(part * LANES, LANES)
        conv = back[:, part * OWN : (part + 1) * OWN, :].reshape(chans, LANES).T
        mixed = gate[at, :] * (conv + skip[...] * gated[at, :])
        yg[own, at, :] = mixed.astype(BF16)
        for to in order:
            y_push(own, part, to)
    for h in range(2):
        y_push(own, h, two2, only=0)

    def mix(block):
        at = pl.ds(pl.multiple_of(block * chans, chans), chans)
        return dot(yg[block], wo[at, :])

    acc[...] = mix(own)
    y_pull(own2, 0), y_push(own2, 0, plus)
    y_pull(own2, 1), y_push(own2, 1, minus)
    y_pull(minus, 0), y_push(minus, 0, plus)
    y_pull(plus, 1), y_push(plus, 1, minus)
    y_pull(minus, 1), y_push(minus, 1, own2)
    y_pull(plus, 0), y_push(plus, 0, own2)
    for block in (own2, minus, plus):
        acc[...] += mix(block)
    y_pull(minus2, 0), y_push(minus2, 0, plus, only=1)
    y_pull(plus2, 1), y_push(plus2, 1, minus, only=1)
    for block, waits in ((two, (0, 1)), (minus2, (1,)), (plus2, (0,)), (two2, (0, 1))):
        for h in waits:
            y_pull(block, h)
        acc[...] += mix(block)
    out_ref[...] = acc[...].astype(BF16)

    x_finish()
    y_finish()
    to_next.wait_send()
    pltpu.make_async_copy(others, others, tail_sem.at[0]).wait()
    whole(hsend, h_sem.at[0]).wait()
    whole(gsend, g_sem.at[0]).wait()
    whole(csend, c_sem.at[0]).wait()


def shards(nctx, nch, inputs, in_weight, short_kernel, long_filter, skip_gain, out_weight):
    rows, feats = inputs.shape
    width, _, chans = in_weight.shape
    mixed = out_weight.shape[1]
    length = rows * nctx
    consts = [jnp.asarray(t) for t in tables(length)]
    k1 = length // LANES
    operands = [
        inputs, jnp.transpose(in_weight, (1, 0, 2)), short_kernel, long_filter,
        skip_gain.reshape(1, chans), out_weight, *consts,
    ]
    vm = pltpu.VMEM
    parts = (nctx, 2 * OWN, LANES)
    scratch = [
        vm((nch, rows, feats), BF16), vm((3, width, chans), BF16), vm(short_kernel.shape, F32),
        vm((rows, chans), F32), vm((1, chans), F32), vm(out_weight.shape, BF16),
        *[vm(c.shape, c.dtype) for c in consts],
        vm((rows + 8, 3 * chans), F32), vm((rows, chans), F32), vm((rows, chans), F32),
        vm(parts, F32), vm(parts, F32), vm(parts, BF16), vm(parts, BF16), vm(parts, BF16), vm(parts, BF16),
        vm((nch, rows, chans), BF16),
        vm((k1 * OWN, LANES), F32), vm((k1 * OWN, 2 * LANES), F32), vm((k1 * OWN, 2 * LANES), F32),
        vm((k1 * OWN, 6 * LANES), BF16), vm((rows, mixed), F32),
        vm((2 * feats // LANES, LANES), F32), vm((nch, 2 * feats // LANES, LANES), F32), vm((8, width), F32),
    ]
    dma = pltpu.SemaphoreType.DMA
    sems = [
        pltpu.SemaphoreType.REGULAR((5,)), dma((10,)), dma((18,)), dma((nch, 2)), dma((2,)), dma((2,)), dma((2,)), dma((2,)), dma((2,)),
        dma((16,)), dma((nch, 2)),
    ]
    return pl.pallas_call(
        functools.partial(kernel, nctx, nch, 2),
        out_shape=pltpu.VMEM((rows, mixed), BF16),
        in_specs=[pl.BlockSpec(memory_space=pltpu.HBM)] * len(operands),
        out_specs=pl.BlockSpec(memory_space=pltpu.VMEM),
        scratch_shapes=scratch + sems,
        compiler_params=pltpu.CompilerParams(
            collective_id=0, has_side_effects=True, vmem_limit_bytes=60 * 1024 * 1024
        ),
    )(*[pltpu.with_memory_space_constraint(o, pltpu.HBM) for o in operands])


def solution(mesh):
    placed = (
        P("ctx", "ch"),
        P(None, None, "ch"),
        P(None, None, "ch"),
        P("ctx", "ch"),
        P("ch"),
        P(None, "ch"),
    )
    body = functools.partial(shards, mesh.shape["ctx"], mesh.shape["ch"])
    return jax.shard_map(body, mesh=mesh, in_specs=placed, out_specs=P("ctx", "ch"), check_vma=False)
```

```python
import functools
import math

import jax
import jax.numpy as jnp
import ml_dtypes
import numpy as np
from jax import lax
from jax.experimental import pallas as pl
from jax.experimental.pallas import tpu as pltpu
from jax.sharding import PartitionSpec as P

MESH = pl.DeviceIdType.MESH
BF16 = jnp.bfloat16
F32 = jnp.float32
LANES = 128
OWN = 8


def halves(table):
    high = table.astype(ml_dtypes.bfloat16)
    low = (table - high.astype(np.float64)).astype(ml_dtypes.bfloat16)
    return np.stack([high, low])


def tables(length):
    rows = length // LANES
    k1 = np.arange(rows)[:, None] + 0.5
    n1 = np.arange(rows)[None, :]
    n2 = np.arange(LANES)[None, :]
    k2 = np.arange(LANES)[:, None]
    outer = 2.0 * math.pi * k1 * n1 / (2 * rows)
    first = np.concatenate([np.cos(outer), -np.sin(outer)], 0)
    turn = 2.0 * math.pi * k1 * n2 / (2 * length)
    twist = np.stack([np.cos(turn), -np.sin(turn)]).astype(np.float32)
    inner = 2.0 * math.pi * k2 * n2 / LANES
    cosine, sine = np.cos(inner), np.sin(inner)
    second = np.block([[cosine, -sine], [sine, cosine]])
    back = np.block([[cosine, sine], [-sine, cosine]])
    return (
        np.concatenate(list(halves(first)), 1),
        np.concatenate([halves(first.T / length)[i] for i in (0, 1, 0)], 1),
        np.stack([np.concatenate([halves(t)[i] for i in (0, 0, 1)]) for t in (second, back)]),
        twist,
    )


def ctx_order(count):
    size = (2, count // 4, 2) if count >= 4 else (1, 1, count)
    nz = size[1]
    far = sorted(range(nz), key=lambda z: -min(z, nz - z))
    every = [(y, z, c) for z in far for y in reversed(range(size[0])) for c in reversed(range(size[2]))]
    return size, [offset for offset in every if offset != (0, 0, 0)]


def split(value):
    high = value.astype(BF16)
    return high, (value - high.astype(F32)).astype(BF16)


def dot(left, right):
    return jnp.dot(left, right, preferred_element_type=F32)


def kernel(nctx, nch, ny, *refs):
    (
        x_hbm, w_hbm, taps_hbm, filt_hbm, skip_hbm, wo_hbm,
        first_hbm, last_hbm, mid_hbm, twist_hbm,
        out_ref,
        xg, w, taps, filt, skip, wo, first, last, mid, twist,
        proj, gate, gated, hsend, hrecv, gsend, grecv, csend, crecv, yg,
        line, spec, hspec, parts3, acc, tail_out, tails, tail_x,
        heard, local_sem, x_send, x_recv, halo_sem, tail_sem, h_sem, g_sem, c_sem, y_send, y_recv,
    ) = refs
    ctx = lax.axis_index("ctx")
    ch = lax.axis_index("ch")
    rows, feats = x_hbm.shape
    chans = filt_hbm.shape[1]
    k1 = first_hbm.shape[0] // 2

    nx = nch // ny
    half = rows // 2

    def at_ch(dx, dy):
        return ((ch // ny + dx) % nx) * ny + (ch % ny + dy) % ny

    own, plus, minus, two = at_ch(0, 0), at_ch(1, 0), at_ch(nx - 1, 0), at_ch(2, 0)
    own2, plus2, minus2, two2 = at_ch(0, 1), at_ch(1, 1), at_ch(nx - 1, 1), at_ch(2, 1)

    size, offsets = ctx_order(nctx)

    def ctx_peer(offset):
        low = ctx % size[2]
        z = (ctx // size[2]) % size[1]
        y = ctx // (size[1] * size[2])
        dy, dz, dc = offset
        return (((y + dy) % size[0]) * size[1] + (z + dz) % size[1]) * size[2] + (low + dc) % size[2]

    ctx_peers = [ctx_peer(offset) for offset in offsets]

    pairs = (
        (x_hbm, xg.at[own]), (filt_hbm, filt), (first_hbm, first), (mid_hbm, mid), (twist_hbm, twist),
        (w_hbm, w), (last_hbm, last), (taps_hbm, taps), (skip_hbm, skip), (wo_hbm, wo),
    )
    local = [pltpu.make_async_copy(s, d, local_sem.at[i]) for i, (s, d) in enumerate(pairs)]
    ways = [(0, 0, 1)] if size[2] > 1 else []
    z_ways = [(0, 1, 0), (0, size[1] - 1, 0)] if size[1] > 1 else []
    y_ways = [(1, 0, 0)] if size[0] > 1 else []
    barrier = pltpu.get_barrier_semaphore()

    def greet(sem, chs, offs):
        for to in chs:
            pl.semaphore_signal(sem, inc=1, device_id={"ch": to}, device_id_type=MESH)
        for offset in offs:
            pl.semaphore_signal(sem, inc=1, device_id={"ctx": ctx_peer(offset)}, device_id_type=MESH)

    near = (plus, minus, own2)
    rounds = [(near, ways), ((own2,), z_ways)] + [((), z_ways)] * 3

    def tell(i):
        greet(heard.at[i], *rounds[i])

    def hear(i):
        count = len(rounds[i][0]) + len(rounds[i][1])
        if count:
            pl.semaphore_wait(heard.at[i], count)

    local[0].start()
    greet(barrier, near, ways + y_ways + z_ways)
    for copy in local[1:]:
        copy.start()

    def to_parts(block):
        turned = block.T.reshape(nctx, OWN, rows)
        return jnp.concatenate([turned[:, :, :LANES], turned[:, :, LANES:]], axis=1)

    pl.semaphore_wait(barrier, len(near) + len(ways + y_ways + z_ways))


    core = ctx % size[2]

    def on(only, act):
        if only is None:
            act()
        else:
            pl.when(core == only)(act)

    def gather(source, slots, send, recv):
        started = []

        def piece(block, h):
            return slots.at[block, pl.ds(h * half, half)]

        def push(block, h, to, src=None, only=None):
            copy = pltpu.make_async_remote_copy(
                src_ref=piece(block, h) if src is None else src.at[pl.ds(h * half, half)],
                dst_ref=piece(block, h), send_sem=send.at[len(started)], recv_sem=recv.at[block, h],
                device_id={"ch": to}, device_id_type=MESH,
            )
            on(only, copy.start)
            started.append((only, copy))

        def pull(block, h, only=None):
            copy = pltpu.make_async_remote_copy(
                src_ref=piece(block, h), dst_ref=piece(block, h), send_sem=send.at[0], recv_sem=recv.at[block, h],
                device_id={"ch": own2}, device_id_type=MESH,
            )
            on(only, copy.wait_recv)

        def finish():
            for only, copy in started:
                on(only, copy.wait_send)

        return push, pull, finish

    local[0].wait()
    x_push, x_pull, x_finish = gather(x_hbm, xg, x_send, x_recv)
    for h, to in ((0, own2), (0, plus), (1, minus), (1, own2), (1, plus), (0, minus)):
        x_push(own, h, to)
    to_next = pltpu.make_async_remote_copy(
        src_ref=tail_out, dst_ref=tails.at[own], send_sem=halo_sem.at[0], recv_sem=halo_sem.at[1],
        device_id={"ctx": (ctx + 1) % nctx}, device_id_type=MESH,
    )
    tell(0)
    local[1].wait()
    hsend[...] = to_parts(filt[...])
    tiles = feats // LANES
    last_rows = xg[own, pl.ds(rows - 16, 16), :].astype(F32)
    for r in range(2):
        for part in range(tiles):
            tail_out[pl.ds(r * tiles + part, 1), :] = last_rows[14 + r : 15 + r, part * LANES : (part + 1) * LANES]
    hear(0)
    tell(1)
    hear(1)
    tell(2)
    to_next.start()


    def exchange(send, recv, sem):
        for to in ctx_peers:
            pltpu.make_async_remote_copy(
                src_ref=send.at[to], dst_ref=recv.at[ctx], send_sem=sem.at[0], recv_sem=sem.at[1],
                device_id={"ctx": to}, device_id_type=MESH,
            ).start()
        recv[pl.ds(ctx, 1)] = send[pl.ds(ctx, 1)]

    def whole(send, sem):
        part = send.at[pl.ds(0, nctx - 1)]
        return pltpu.make_async_copy(part, part, sem)

    def lay(at, col, value):
        high, low = split(value)
        for i, half_value in enumerate((high, low, high)):
            parts3[at, col + 2 * LANES * i : col + 2 * LANES * i + LANES] = half_value

    def forward(result, exact):
        block = jnp.concatenate([line[pl.ds(c, k1, stride=OWN), :] for c in range(OWN)], axis=1)
        high, low = split(block)
        turned = dot(first[...], jnp.concatenate([high, high], axis=0))
        if not exact:
            turned = turned + dot(first[...], jnp.concatenate([low, jnp.zeros_like(low)], axis=0))
        for c in range(OWN):
            real = turned[:k1, c * LANES : (c + 1) * LANES]
            imag = turned[k1:, c * LANES : (c + 1) * LANES]
            at = pl.ds(c * k1, k1)
            lay(at, 0, real * twist[0] - imag * twist[1])
            lay(at, LANES, real * twist[1] + imag * twist[0])
        result[...] = dot(parts3[...], mid[0])

    def backward():
        xr, xi = spec[:, :LANES], spec[:, LANES:]
        hr, hi = hspec[:, :LANES], hspec[:, LANES:]
        every = slice(None)
        lay(every, 0, xr * hr - xi * hi)
        lay(every, LANES, xr * hi + xi * hr)
        spec[...] = dot(parts3[...], mid[1])
        cols = []
        for c in range(OWN):
            at = pl.ds(c * k1, k1)
            real, imag = spec[at, :LANES], spec[at, LANES:]
            cols.append(
                jnp.concatenate([real * twist[0] + imag * twist[1], imag * twist[0] - real * twist[1]], axis=0)
            )
        high, low = split(jnp.concatenate(cols, axis=1))
        signal = dot(last[...], jnp.concatenate([high, high, low], axis=0))
        for c in range(OWN):
            line[pl.ds(c, k1, stride=OWN), :] = signal[:, c * LANES : (c + 1) * LANES]

    top = 8

    def project(block, first_one=False):
        part = xg[block]
        at = pl.ds(pl.multiple_of(block * feats, feats), feats)
        for s in range(3):
            cols = pl.ds(s * chans, chans)
            term = dot(part, w[s, at, :])
            proj[top:, cols] = term if first_one else proj[top:, cols] + term

    x_pull(minus, 0), x_push(minus, 0, plus), x_push(minus, 0, own2, only=0)
    x_pull(plus, 1), x_push(plus, 1, minus), x_push(plus, 1, own2, only=0)
    hear(2)
    tell(3)
    x_pull(own2, 0, only=1), x_push(own2, 0, plus, only=1), x_push(own2, 0, minus, only=1)
    x_pull(own2, 1, only=1), x_push(own2, 1, minus, only=1), x_push(own2, 1, plus, only=1)
    hear(3)
    tell(4)
    to_next.wait_recv()
    to_ch = [
        pltpu.make_async_remote_copy(
            src_ref=tails.at[own], dst_ref=tails.at[own], send_sem=tail_sem.at[0], recv_sem=tail_sem.at[1],
            device_id={"ch": (ch + step) % nch}, device_id_type=MESH,
        )
        for step in range(1, nch)
    ]
    for copy in to_ch:
        copy.start()
    x_pull(minus, 1, only=0), x_push(minus, 1, own2, only=0)
    x_pull(plus, 0, only=0), x_push(plus, 0, own2, only=0)
    for h in range(2):
        x_pull(two, h), x_push(two, h, own2, only=1)
    hear(4)
    for copy in local[2:]:
        copy.wait()
    project(own, True)
    x_pull(own2, 0, only=0), x_pull(own2, 1, only=0)
    project(own2)

    x_pull(minus2, 0), x_push(minus2, 0, plus, only=0)
    x_pull(plus2, 1), x_push(plus2, 1, minus, only=0)
    exchange(hsend, hrecv, h_sem)
    others = tails.at[pl.ds(0, nch - 1)]
    pltpu.make_async_copy(others, others, tail_sem.at[1]).wait()
    tail_x[...] = jnp.zeros_like(tail_x)
    for block in range(nch):
        for r in range(2):
            for part in range(tiles):
                at = pl.ds(block * feats + part * LANES, LANES)
                tail_x[pl.ds(top - 2 + r, 1), at] = tails[block, pl.ds(r * tiles + part, 1), :]
    for s in range(3):
        before = dot(tail_x[...].astype(BF16), w[s])
        proj[:top, pl.ds(s * chans, chans)] = jnp.where(ctx == 0, 0.0, before)
    x_pull(minus, 1, only=1), x_pull(plus, 0, only=1)
    for block in (two, minus, plus):
        project(block)
    for block, waits in ((minus2, (1,)), (plus2, (0,)), (two2, (0, 1))):
        for h in waits:
            x_pull(block, h)
        project(block)
    def stream(s):
        cols = pl.ds(s * chans, chans)
        return (
            taps[0, s : s + 1, :] * proj[top:, cols]
            + taps[1, s : s + 1, :] * proj[pl.ds(top - 1, rows), cols]
            + taps[2, s : s + 1, :] * proj[pl.ds(top - 2, rows), cols]
        )

    gated[...] = stream(0) * stream(2)
    gsend[...] = to_parts(gated[...]).astype(BF16)
    exchange(gsend, grecv, g_sem)
    gate[...] = stream(1)
    whole(hsend, h_sem.at[1]).wait()
    line[...] = hrecv[...].reshape(line.shape)
    forward(hspec, False)
    whole(gsend, g_sem.at[1]).wait()

    line[...] = grecv[...].astype(F32).reshape(line.shape)
    forward(spec, True)
    backward()
    csend[...] = line[...].reshape(csend.shape).astype(BF16)
    exchange(csend, crecv, c_sem)
    whole(csend, c_sem.at[1]).wait()
    y_push, y_pull, y_finish = gather(yg.at[own], yg, y_send, y_recv)
    back = crecv[...].astype(F32)
    for part, order in ((0, (own2, plus, minus)), (1, (own2, minus, plus))):
        at = pl.ds(part * LANES, LANES)
        conv = back[:, part * OWN : (part + 1) * OWN, :].reshape(chans, LANES).T
        mixed = gate[at, :] * (conv + skip[...] * gated[at, :])
        yg[own, at, :] = mixed.astype(BF16)
        for to in order:
            y_push(own, part, to)
    for h in range(2):
        y_push(own, h, two2, only=0)

    def mix(block):
        at = pl.ds(pl.multiple_of(block * chans, chans), chans)
        return dot(yg[block], wo[at, :])

    acc[...] = mix(own)
    y_pull(own2, 0), y_push(own2, 0, plus)
    y_pull(own2, 1), y_push(own2, 1, minus)
    y_pull(minus, 0), y_push(minus, 0, plus)
    y_pull(plus, 1), y_push(plus, 1, minus)
    y_pull(minus, 1), y_push(minus, 1, own2)
    y_pull(plus, 0), y_push(plus, 0, own2)
    for block in (own2, minus, plus):
        acc[...] += mix(block)
    y_pull(minus2, 0), y_push(minus2, 0, plus, only=1)
    y_pull(plus2, 1), y_push(plus2, 1, minus, only=1)
    for block, waits in ((two, (0, 1)), (minus2, (1,)), (plus2, (0,)), (two2, (0, 1))):
        for h in waits:
            y_pull(block, h)
        acc[...] += mix(block)
    out_ref[...] = acc[...].astype(BF16)

    x_finish()
    y_finish()
    to_next.wait_send()
    pltpu.make_async_copy(others, others, tail_sem.at[0]).wait()
    whole(hsend, h_sem.at[0]).wait()
    whole(gsend, g_sem.at[0]).wait()
    whole(csend, c_sem.at[0]).wait()


def shards(nctx, nch, inputs, in_weight, short_kernel, long_filter, skip_gain, out_weight):
    rows, feats = inputs.shape
    width, _, chans = in_weight.shape
    mixed = out_weight.shape[1]
    length = rows * nctx
    consts = [jnp.asarray(t) for t in tables(length)]
    k1 = length // LANES
    operands = [
        inputs, jnp.transpose(in_weight, (1, 0, 2)), short_kernel, long_filter,
        skip_gain.reshape(1, chans), out_weight, *consts,
    ]
    vm = pltpu.VMEM
    parts = (nctx, 2 * OWN, LANES)
    scratch = [
        vm((nch, rows, feats), BF16), vm((3, width, chans), BF16), vm(short_kernel.shape, F32),
        vm((rows, chans), F32), vm((1, chans), F32), vm(out_weight.shape, BF16),
        *[vm(c.shape, c.dtype) for c in consts],
        vm((rows + 8, 3 * chans), F32), vm((rows, chans), F32), vm((rows, chans), F32),
        vm(parts, F32), vm(parts, F32), vm(parts, BF16), vm(parts, BF16), vm(parts, BF16), vm(parts, BF16),
        vm((nch, rows, chans), BF16),
        vm((k1 * OWN, LANES), F32), vm((k1 * OWN, 2 * LANES), F32), vm((k1 * OWN, 2 * LANES), F32),
        vm((k1 * OWN, 6 * LANES), BF16), vm((rows, mixed), F32),
        vm((2 * feats // LANES, LANES), F32), vm((nch, 2 * feats // LANES, LANES), F32), vm((8, width), F32),
    ]
    dma = pltpu.SemaphoreType.DMA
    sems = [
        pltpu.SemaphoreType.REGULAR((5,)), dma((10,)), dma((20,)), dma((nch, 2)), dma((2,)), dma((2,)), dma((2,)), dma((2,)), dma((2,)),
        dma((16,)), dma((nch, 2)),
    ]
    return pl.pallas_call(
        functools.partial(kernel, nctx, nch, 2),
        out_shape=pltpu.VMEM((rows, mixed), BF16),
        in_specs=[pl.BlockSpec(memory_space=pltpu.HBM)] * len(operands),
        out_specs=pl.BlockSpec(memory_space=pltpu.VMEM),
        scratch_shapes=scratch + sems,
        compiler_params=pltpu.CompilerParams(
            collective_id=0, has_side_effects=True, vmem_limit_bytes=60 * 1024 * 1024
        ),
    )(*[pltpu.with_memory_space_constraint(o, pltpu.HBM) for o in operands])


def solution(mesh):
    placed = (
        P("ctx", "ch"),
        P(None, None, "ch"),
        P(None, None, "ch"),
        P("ctx", "ch"),
        P("ch"),
        P(None, "ch"),
    )
    body = functools.partial(shards, mesh.shape["ctx"], mesh.shape["ch"])
    return jax.shard_map(body, mesh=mesh, in_specs=placed, out_specs=P("ctx", "ch"), check_vma=False)
```
